256 devices in a mesh: tm: 4 (over x_lo, core), space: 64 (over x_hi, z, y).
Axes of the slice: x: 4 (x_hi: 2, x_lo: 2; x = x_hi * 2 + x_lo), y: 4, z: 8, core: 2. Of those that a mesh axis runs over, the one named last changes fastest.
Arguments:
- obs_perturb: bfloat16 [4, 256, 1024, 256], P('tm', 'space'), may hold values from -1.796875 to 1.796875
- innovation: float32 [4, 256, 1024], P('tm', 'space'), may hold values from -12 to 12
- error_weight: float32 [4, 256, 1024], P('tm', 'space'), may hold values from 0.5 to 2
- obs_column: int32 [4, 256, 1024], P('tm', 'space'), may hold values from 0 to 31
- obs_count: int32 [4, 256], P('tm', 'space'), may hold values from 64 to 1024, as said below
- radius: int32 [256], P('space'), may hold values from 56 to 80
- states: bfloat16 [8, 8192, 16, 256], P('tm', 'space'), may hold values from -6 to 6
Outputs:
- analysis: bfloat16 [8, 8192, 16, 256], P('tm', 'space')
The draws below stay inside these ranges and needn't reach their ends.
Inputs may be any that keep to these rules, and one draw needn't show every extreme that they name: `obs_count`: at most 1024; some slot and region holds exactly 1024 in every draw.
All inputs are finite; a program needn't handle non-finite values.
Results may differ from the reference program's by a relative error of at most 0.0065.
Values may be sent and summed in bfloat16 or wider, within the bound.
No kernel may reach another device: no remote copies, remote signals or barrier semaphores. Data moves between devices by JAX's collectives and lax.ppermute only.
A program may use at most 64 MiB of HBM per device.

```python
import math
import jax
import jax.numpy as jnp
from jax import lax

K = 256
HC = 32
LEV = 16
OBS_CAP = 1024
NS_ITERS = 5
SLOTS = 4
LAGS = 8
REGIONS = 256
COLUMNS = 8192


def draw_obs_count(key, part):
    heavy_key, high_key, low_key, pick_key = jax.random.split(key, 4)
    grid_shape = (SLOTS, REGIONS)
    heavy_mask = jax.random.randint(heavy_key, grid_shape, 0, 4) == 0
    high_count = jax.random.randint(high_key, grid_shape, OBS_CAP // 2, OBS_CAP + 1)
    low_count = jax.random.randint(low_key, grid_shape, OBS_CAP // 16, OBS_CAP // 4 + 1)
    counts = jnp.where(heavy_mask, high_count, low_count).reshape(-1)
    chosen = jax.random.randint(pick_key, (), 0, SLOTS * REGIONS)
    counts = counts.at[chosen].set(OBS_CAP)
    return counts.reshape(grid_shape).astype(jnp.int32)


def place_ends(drawn, own_key, smallest, top_value):
    dims = drawn.shape
    place = [jax.random.randint(jax.random.fold_in(own_key, axis), (), 0, dims[axis]) for axis in range(len(dims))]
    drawn = drawn.at[tuple(place)].set(smallest)
    longest = dims.index(max(dims))
    place[longest] = (place[longest] + 1) % dims[longest]
    return drawn.at[tuple(place)].set(top_value)


def shard_levels(rng, dims, pieces, low, largest):
    level = 1.0
    for dim, blocks in pieces:
        draws = jax.random.uniform(jax.random.fold_in(jax.random.fold_in(rng, 6), dim), (blocks,), jnp.float32, low / len(pieces), largest / len(pieces))
        level = level * jnp.repeat(jnp.exp(draws), dims[dim] // blocks).reshape((-1,) + (1,) * (len(dims) - 1 - dim))
    return level


def centred(stream_key, extent, deviation, reach, pieces=(), held_as=jnp.bfloat16):
    gain = shard_levels(stream_key, extent, pieces, -0.22, 0.18) if pieces else 1.0
    entries = jax.random.normal(stream_key, extent, jnp.float32) * deviation * gain
    return jnp.minimum(jnp.maximum(entries, -reach), reach).astype(held_as)


def setup_inputs(seed: int = 0) -> dict:
    keys = jax.random.split(jax.random.key(seed), 8)
    return {
        "obs_perturb": centred(keys[0], (SLOTS, REGIONS, OBS_CAP, K), 0.3, 1.796875, ((0, 4), (1, 64))),
        "innovation": centred(keys[1], (SLOTS, REGIONS, OBS_CAP), 2.0, 12.0, ((0, 4), (1, 64)), jnp.float32),
        "error_weight": jnp.clip(jnp.exp(math.log(2.0) - 1.3862944 * jax.random.uniform(keys[2], (SLOTS, REGIONS, OBS_CAP), jnp.float32) ** shard_levels(keys[2], (SLOTS, REGIONS, OBS_CAP), ((0, 4), (1, 64)), -0.2, 0.2)), 0.5, 2.0),
        "obs_column": place_ends(jax.random.randint(keys[3], (SLOTS, REGIONS, OBS_CAP), 0, HC), jax.random.fold_in(keys[3], 1), 0, HC - 1).astype(jnp.int32),
        "obs_count": draw_obs_count(jax.random.fold_in(keys[7], 71), 0),
        "radius": place_ends(jax.random.randint(keys[5], (REGIONS,), 7 * HC // 4, 5 * HC // 2 + 1), jax.random.fold_in(keys[5], 1), 7 * HC // 4, (5 * HC // 2 + 1) - 1).astype(jnp.int32),
        "states": centred(keys[6], (LAGS, COLUMNS, LEV, K), 1.0, 6.0, ((0, 4), (1, 64))),
    }


INFLATION = 1.1
HIGHEST = lax.Precision.HIGHEST

def taper(column, radius, offset, width):
    distance = jnp.abs(column.astype(jnp.float32) + 0.5 - 0.5 * width - offset * width)
    ratio = jnp.minimum(distance / radius.astype(jnp.float32), 1.0)
    return jnp.square(1.0 - ratio * ratio)

def ensemble_transform(gram_sum, innov_sum):
    members = gram_sum.shape[-1]
    identity = jnp.eye(members, dtype=jnp.float32)
    system = gram_sum + (members - 1) / INFLATION * identity
    frobenius = jnp.sqrt(lax.optimization_barrier(jnp.sum(system * system, axis=(1, 2))))
    root_now = system / frobenius[:, None, None]
    inverse = jnp.broadcast_to(identity, system.shape)
    for iteration in range(NS_ITERS):
        middle = 1.5 * identity - 0.5 * jnp.einsum('nij,njk->nik', inverse, root_now, precision=HIGHEST)
        root_now = jnp.einsum('nij,njk->nik', root_now, middle, precision=HIGHEST)
        inverse = jnp.einsum('nij,njk->nik', middle, inverse, precision=HIGHEST)
    spread_part = jnp.sqrt(members - 1.0) * inverse / jnp.sqrt(frobenius)[:, None, None]
    half_step = jnp.einsum('nij,nj->ni', inverse, innov_sum, precision=HIGHEST)
    mean_part = jnp.einsum('nij,nj->ni', inverse, half_step, precision=HIGHEST) / frobenius[:, None]
    return spread_part + mean_part[:, :, None]

def reference(obs_perturb, innovation, error_weight, obs_column, obs_count, radius, states):
    slot_count, region_count, capacity, members = obs_perturb.shape
    position = lax.broadcasted_iota(jnp.int32, (slot_count, region_count, capacity), 2)
    present = (position < obs_count[:, :, None]).astype(jnp.float32)
    base_weight = error_weight * present
    weights = jnp.stack([base_weight * taper(obs_column, radius[None, :, None], offset, HC) for offset in range(-2, 3)])

    def region_gram(target):
        gram_sum = jnp.zeros((members, members), jnp.float32)
        vec_sum = jnp.zeros((members,), jnp.float32)
        for term_index, offset in enumerate(range(-2, 3)):
            source = (target - offset) % region_count
            source_rows = obs_perturb[:, source].reshape(-1, members)
            weight = weights[term_index][:, source].reshape(-1)
            weighted = (source_rows * weight[:, None]).astype(jnp.bfloat16)
            gram_sum = gram_sum + jnp.dot(weighted.T, source_rows, preferred_element_type=jnp.float32)
            vec_sum = vec_sum + jnp.dot(weighted.astype(jnp.float32).T, innovation[:, source].reshape(-1), precision=HIGHEST)
        return (gram_sum, vec_sum)
    gram_all, vec_all = lax.map(region_gram, jnp.arange(region_count, dtype=jnp.int32))
    transform = ensemble_transform(gram_all, vec_all).astype(jnp.bfloat16)
    preceding = jnp.roll(transform, 1, axis=0)
    following = jnp.roll(transform, -1, axis=0)
    lag_count = states.shape[0]
    levels = states.shape[2]
    shaped = states.reshape(lag_count, region_count, HC, levels, members)
    half_width = HC // 2
    blend_weight = jnp.abs((jnp.arange(HC, dtype=jnp.float32) + 0.5) / HC - 0.5).reshape(1, HC, 1, 1)

    def region_update(target):
        region_state = shaped[:, target]
        mean_state = lax.optimization_barrier(jnp.mean(region_state.astype(jnp.float32), axis=-1, keepdims=True))
        anomaly = (region_state - mean_state).astype(jnp.bfloat16)
        centre = jnp.dot(anomaly.reshape(-1, members), transform[target], preferred_element_type=jnp.float32)
        centre = centre.reshape(lag_count, HC, levels, members)
        western = jnp.dot(anomaly[:, :half_width].reshape(-1, members), preceding[target], preferred_element_type=jnp.float32)
        eastern = jnp.dot(anomaly[:, half_width:].reshape(-1, members), following[target], preferred_element_type=jnp.float32)
        beside = jnp.concatenate([western.reshape(lag_count, half_width, levels, members), eastern.reshape(lag_count, HC - half_width, levels, members)], axis=1)
        return (mean_state + (1.0 - blend_weight) * centre + blend_weight * beside).astype(jnp.bfloat16)
    updated = lax.map(region_update, jnp.arange(region_count, dtype=jnp.int32))
    return jnp.moveaxis(updated, 0, 1).reshape(states.shape)
```

```python
import functools

import jax
import jax.numpy as jnp
from jax import lax
from jax.experimental import pallas as pl
from jax.experimental.pallas import tpu as pltpu
from jax.sharding import PartitionSpec as P

HC = 32
NS_ITERS = 5
INFLATION = 1.1
K = 256
HALF = K // 2
ROWS = HALF + HALF + 16
BF16 = jnp.bfloat16
F32 = jnp.float32
VMEM_LIMIT = 48 * 1024 * 1024


def row_col():
    row = lax.broadcasted_iota(jnp.int32, (HALF, HALF), 0)
    col = lax.broadcasted_iota(jnp.int32, (HALF, HALF), 1)
    return row, col


def tail_row():
    return lax.broadcasted_iota(jnp.int32, (16, HALF), 0)


def gram_kernel(core_ref, count_ref, radius_ref, obs_ref, innov_ref, error_ref, column_ref,
                send_ref, keep_ref, acc_ref, vec_ref):
    region = pl.program_id(0)
    capacity = obs_ref.shape[2]

    @pl.when(region == 0)
    def _():
        acc_ref[...] = jnp.zeros_like(acc_ref)
        vec_ref[...] = jnp.zeros_like(vec_ref)

    obs = obs_ref[0, 0]
    obs_t = obs.T.astype(F32)
    here = pl.ds(region, 1)
    column = column_ref[0, here, :].astype(F32)
    offset = lax.broadcasted_iota(jnp.int32, (8, capacity), 0).astype(F32) - 2.0
    position = lax.broadcasted_iota(jnp.int32, (1, capacity), 1)
    base = jnp.where(position < count_ref[0, region], error_ref[0, here, :], 0.0)
    radius = radius_ref[region].astype(F32)
    distance = jnp.abs(column + (0.5 - 0.5 * HC) - offset * HC)
    ratio = jnp.minimum(distance / radius, 1.0)
    weight = base * jnp.square(1.0 - ratio * ratio)
    scaled = weight * innov_ref[0, here, :]
    scaled_high = scaled.astype(BF16)
    scaled_low = (scaled - scaled_high.astype(F32)).astype(BF16)
    vec = jnp.dot(jnp.concatenate([scaled_high, scaled_low], axis=0), obs,
                  preferred_element_type=F32)
    vec = vec[:8] + vec[8:]
    for m in range(5):
        weighted = (obs_t * weight[m : m + 1]).astype(BF16)
        target = pl.ds(pl.multiple_of((region + m) * K, K), K)
        acc_ref[target, :] += jnp.dot(weighted, obs, preferred_element_type=F32)
        vec_ref[pl.ds(region + m, 1), :] += vec[m : m + 1]

    @pl.when(region == pl.num_programs(0) - 1)
    def _():
        row, col = row_col()
        tail = tail_row()
        core = core_ref[0]
        for start, out_ref in (((1 - core) * 4, send_ref), (core * 4, keep_ref)):
            for k in range(4):
                at = pl.multiple_of((start + k) * K, K)
                top = acc_ref[pl.ds(at, HALF), :]
                low = acc_ref[pl.ds(at + HALF, HALF), HALF:]
                out_ref[k, :HALF, :] = top[:, HALF:].astype(out_ref.dtype)
                out_ref[k, HALF:K, :] = jnp.where(row <= col, top[:, :HALF], low).astype(out_ref.dtype)
                diag = jnp.sum(jnp.where(row == col, low, 0.0), axis=0, keepdims=True)
                v = vec_ref[pl.ds(start + k, 1), :]
                rest = jnp.where(tail == 0, diag, jnp.where(tail == 1, v[:, :HALF], jnp.where(tail == 2, v[:, HALF:], 0.0)))
                out_ref[k, K:, :] = rest.astype(out_ref.dtype)


def local_grams(core, obs_perturb, innovation, error_weight, obs_column, obs_count, radius):
    _, regions, capacity, members = obs_perturb.shape
    smem = pl.BlockSpec(memory_space=pltpu.SMEM)
    whole = pl.BlockSpec((1, regions, capacity), lambda r: (0, 0, 0))
    out = pl.BlockSpec((4, ROWS, HALF), lambda r: (0, 0, 0))
    return pl.pallas_call(
        gram_kernel,
        grid=(regions,),
        in_specs=[smem, smem, smem,
                  pl.BlockSpec((1, 1, capacity, members), lambda r: (0, r, 0, 0)),
                  whole, whole, whole],
        out_specs=[out, out],
        out_shape=[jax.ShapeDtypeStruct((4, ROWS, HALF), BF16),
                   jax.ShapeDtypeStruct((4, ROWS, HALF), F32)],
        scratch_shapes=[pltpu.VMEM(((regions + 4) * K, K), F32), pltpu.VMEM((regions + 4, K), F32)],
        compiler_params=pltpu.CompilerParams(vmem_limit_bytes=VMEM_LIMIT),
        cost_estimate=pl.CostEstimate(flops=10 * regions * capacity * K * K,
                                      bytes_accessed=2 * regions * capacity * K, transcendentals=0),
        name="local_grams",
    )(core, obs_count, radius, obs_perturb, innovation, error_weight, obs_column)


def split_kernel(core_ref, keep_ref, recv_ref, send_ref, mine_ref):
    core = core_ref[0]
    for k in range(3):
        send_ref[k] = (keep_ref[core + k] + recv_ref[core + k].astype(F32)).astype(BF16)
        mine_ref[k] = keep_ref[1 - core + k] + recv_ref[1 - core + k].astype(F32)


def split_sums(core, keep, recv):
    vmem = pl.BlockSpec(memory_space=pltpu.VMEM)
    return pl.pallas_call(
        split_kernel,
        in_specs=[pl.BlockSpec(memory_space=pltpu.SMEM), vmem, vmem],
        out_specs=[vmem, vmem],
        out_shape=[jax.ShapeDtypeStruct((3, ROWS, HALF), BF16),
                   jax.ShapeDtypeStruct((3, ROWS, HALF), F32)],
        name="split_sums",
    )(core, keep, recv)


def identity_mask(n):
    return lax.broadcasted_iota(jnp.int32, (n, n), 0) == lax.broadcasted_iota(jnp.int32, (n, n), 1)


def product(a, b):
    return jnp.dot(a.astype(BF16), b.astype(BF16), preferred_element_type=F32)


def transform_kernel(mine_ref, halo_ref, other_ref, out_ref):
    row, col = row_col()
    on_diagonal = identity_mask(K)
    count = mine_ref.shape[0]
    state = []
    for k in range(count):
        packed = mine_ref[k] + halo_ref[k].astype(F32) + other_ref[k].astype(F32)
        corner = packed[:HALF]
        both = packed[HALF:K]
        flipped = both.T
        upper = jnp.where(row <= col, both, flipped)
        lower = jnp.where(row > col, both, jnp.where(row == col, packed[K : K + 1], flipped))
        system = jnp.concatenate(
            [jnp.concatenate([upper, corner], axis=1),
             jnp.concatenate([corner.T, lower], axis=1)], axis=0)
        system = system + jnp.where(on_diagonal, (K - 1) / INFLATION, 0.0)
        vec = jnp.concatenate([packed[K + 1 : K + 2], packed[K + 2 : K + 3]], axis=1)
        frob = jnp.sqrt(jnp.sum(jnp.sum(system * system, axis=0, keepdims=True), axis=1, keepdims=True))
        root = system / frob
        rho = jnp.sum(jnp.sum(jnp.where(on_diagonal, root, 0.0), axis=0, keepdims=True), axis=1, keepdims=True) / K
        state.append((root - jnp.where(on_diagonal, rho, 0.0), rho, None, 1.0, frob, vec))
    for iteration in range(NS_ITERS):
        for k in range(count):
            root, rho, inv, iota, frob, vec = state[k]
            mu = 1.5 - 0.5 * iota * rho
            if inv is None:
                mid = -0.5 * root
            else:
                mid = -0.5 * (iota * root + rho * inv + product(inv, root))
            if iteration < NS_ITERS - 1:
                root = rho * mid + mu * root + product(root, mid)
            if inv is None:
                inv = mid
            else:
                inv = mu * inv + iota * mid + product(mid, inv)
            rho, iota = rho * mu, mu * iota
            state[k] = (root, rho, inv, iota, frob, vec)
    for k in range(count):
        _, _, inv, iota, frob, vec = state[k]
        inverse = inv + jnp.where(on_diagonal, iota, 0.0)
        vec_col = jnp.broadcast_to(vec, (HALF, K)).T[:, :1]
        half_step = jnp.sum(inverse * vec_col, axis=0, keepdims=True)
        wbar = jnp.sum(inverse * half_step, axis=1, keepdims=True) / frob
        scale = (K - 1.0) ** 0.5 / jnp.sqrt(frob)
        out_ref[k] = (scale * inverse + wbar).astype(BF16)


def transforms(mine, halo, other):
    vmem = pl.BlockSpec(memory_space=pltpu.VMEM)
    return pl.pallas_call(
        transform_kernel,
        in_specs=[vmem, vmem, vmem],
        out_specs=vmem,
        out_shape=jax.ShapeDtypeStruct((mine.shape[0], K, K), BF16),
        compiler_params=pltpu.CompilerParams(vmem_limit_bytes=VMEM_LIMIT),
        name="transforms",
    )(mine, halo, other)


def update_kernel(core_ref, mine_ref, other_ref, states_ref, out_ref, all_ref):
    region = pl.program_id(0)

    @pl.when(region == 0)
    def _():
        core = core_ref[0]
        all_ref[pl.ds(3 * core, 3)] = mine_ref[...]
        all_ref[pl.ds(3 * (1 - core), 3)] = other_ref[...]

    lags, columns, levels, members = states_ref.shape
    rows = columns * levels // 2
    for lag in range(lags):
        for side in range(2):
            cols = slice(side * columns // 2, (side + 1) * columns // 2)
            state = states_ref[lag, cols].reshape(rows, members).astype(F32)
            mean = jnp.mean(state, axis=1, keepdims=True)
            anomaly = (state - mean).astype(BF16)
            centre = jnp.dot(anomaly, all_ref[region + 1], preferred_element_type=F32)
            beside = jnp.dot(anomaly, all_ref[region + 2 * side], preferred_element_type=F32)
            column = lax.broadcasted_iota(jnp.int32, (rows, 1), 0) // levels + side * columns // 2
            blend = jnp.abs((column.astype(F32) + 0.5) / columns - 0.5)
            result = mean + centre + blend * (beside - centre)
            out_ref[lag, cols] = result.astype(BF16).reshape(columns // 2, levels, members)


def update(core, mine, other, states):
    lags, columns, levels, members = states.shape
    regions = columns // HC
    whole = pl.BlockSpec((3, K, K), lambda r: (0, 0, 0))
    block = pl.BlockSpec((lags, HC, levels, members), lambda r: (0, r, 0, 0))
    return pl.pallas_call(
        update_kernel,
        grid=(regions,),
        in_specs=[pl.BlockSpec(memory_space=pltpu.SMEM), whole, whole, block],
        out_specs=block,
        out_shape=jax.ShapeDtypeStruct(states.shape, BF16),
        scratch_shapes=[pltpu.VMEM((6, K, K), BF16)],
        compiler_params=pltpu.CompilerParams(vmem_limit_bytes=VMEM_LIMIT),
        name="update",
    )(core, mine, other, states)


def shards(obs_perturb, innovation, error_weight, obs_column, obs_count, radius, states):
    core = (lax.axis_index("tm") % 2).astype(jnp.int32).reshape(1)
    spaces = lax.axis_size("space")
    send, keep = local_grams(core, obs_perturb, innovation, error_weight, obs_column, obs_count, radius)
    swap_core = [(0, 1), (1, 0), (2, 3), (3, 2)]
    swap_chip = [(0, 2), (2, 0), (1, 3), (3, 1)]
    recv = lax.ppermute(send, "tm", swap_core)
    edge, mine = split_sums(core, keep, recv)
    perm = []
    for chip in range(2):
        for s in range(spaces):
            low, high = 2 * chip * spaces, (2 * chip + 1) * spaces
            perm.append((high + s, low + (s + 1) % spaces))
            perm.append((low + s, high + (s - 1) % spaces))
    halo = lax.ppermute(edge, ("tm", "space"), perm)
    chip_sum = (mine + halo.astype(F32)).astype(BF16)
    other_chip = lax.ppermute(chip_sum, "tm", swap_chip)
    own = transforms(mine, halo, other_chip)
    beside = lax.ppermute(own, "tm", swap_core)
    return update(core, own, beside, states)


def solution(mesh):
    return jax.shard_map(
        shards,
        mesh=mesh,
        in_specs=(
            P("tm", "space", None, None),
            P("tm", "space", None),
            P("tm", "space", None),
            P("tm", "space", None),
            P("tm", "space"),
            P("space"),
            P("tm", "space", None, None),
        ),
        out_specs=P("tm", "space", None, None),
        check_vma=False,
    )
```

```python
import functools

import jax
import jax.numpy as jnp
from jax import lax
from jax.experimental import pallas as pl
from jax.experimental.pallas import tpu as pltpu
from jax.sharding import PartitionSpec as P

HC = 32
NS_ITERS = 5
INFLATION = 1.1
K = 256
HALF = K // 2
ROWS = HALF + HALF + 16
BF16 = jnp.bfloat16
F32 = jnp.float32
VMEM_LIMIT = 32 * 1024 * 1024
GRAM_VMEM_LIMIT = 56 * 1024 * 1024


def row_col():
    row = lax.broadcasted_iota(jnp.int32, (HALF, HALF), 0)
    col = lax.broadcasted_iota(jnp.int32, (HALF, HALF), 1)
    return row, col


def tail_row():
    return lax.broadcasted_iota(jnp.int32, (16, HALF), 0)


def gram_kernel(core_ref, count_hbm, radius_hbm, obs_hbm, innov_hbm, error_hbm, column_hbm,
                send_ref, keep_ref, acc_ref, vec_ref, count_ref, radius_ref, obs_ref, innov_ref,
                error_ref, column_ref, small_sems, obs_sems):
    regions, capacity = obs_ref.shape[:2]
    small = [pltpu.make_async_copy(src, dst, small_sems.at[i]) for i, (src, dst) in enumerate(
        [(count_hbm, count_ref), (radius_hbm, radius_ref), (innov_hbm.at[0], innov_ref),
         (error_hbm.at[0], error_ref), (column_hbm.at[0], column_ref)])]
    blocks = [pltpu.make_async_copy(obs_hbm.at[0, r], obs_ref.at[r], obs_sems.at[r])
              for r in range(regions)]
    for copy in small + blocks:
        copy.start()
    acc_ref[...] = jnp.zeros_like(acc_ref)
    vec_ref[...] = jnp.zeros_like(vec_ref)
    for copy in small:
        copy.wait()
    offset = lax.broadcasted_iota(jnp.int32, (8, capacity), 0).astype(F32) - 2.0
    position = lax.broadcasted_iota(jnp.int32, (1, capacity), 1)

    @pl.loop(0, regions)
    def _(region):
        pltpu.make_async_copy(obs_hbm.at[0, region], obs_ref.at[region], obs_sems.at[region]).wait()
        obs = obs_ref[region]
        obs_t = obs.T.astype(F32)
        here = pl.ds(region, 1)
        column = column_ref[here, :].astype(F32)
        base = jnp.where(position < count_ref[0, region], error_ref[here, :], 0.0)
        radius = radius_ref[region].astype(F32)
        distance = jnp.abs(column + (0.5 - 0.5 * HC) - offset * HC)
        ratio = jnp.minimum(distance / radius, 1.0)
        weight = base * jnp.square(1.0 - ratio * ratio)
        scaled = weight * innov_ref[here, :]
        scaled_high = scaled.astype(BF16)
        scaled_low = (scaled - scaled_high.astype(F32)).astype(BF16)
        vec = jnp.dot(jnp.concatenate([scaled_high, scaled_low], axis=0), obs,
                      preferred_element_type=F32)
        vec = vec[:8] + vec[8:]
        for m in range(5):
            weighted = (obs_t * weight[m : m + 1]).astype(BF16)
            target = pl.ds(pl.multiple_of((region + m) * K, K), K)
            acc_ref[target, :] += jnp.dot(weighted, obs, preferred_element_type=F32)
            vec_ref[pl.ds(region + m, 1), :] += vec[m : m + 1]

    row, col = row_col()
    tail = tail_row()
    core = core_ref[0]
    for start, out_ref in (((1 - core) * 4, send_ref), (core * 4, keep_ref)):
        for k in range(4):
            at = pl.multiple_of((start + k) * K, K)
            top = acc_ref[pl.ds(at, HALF), :]
            low = acc_ref[pl.ds(at + HALF, HALF), HALF:]
            out_ref[k, :HALF, :] = top[:, HALF:].astype(out_ref.dtype)
            out_ref[k, HALF:K, :] = jnp.where(row <= col, top[:, :HALF], low).astype(out_ref.dtype)
            diag = jnp.sum(jnp.where(row == col, low, 0.0), axis=0, keepdims=True)
            v = vec_ref[pl.ds(start + k, 1), :]
            rest = jnp.where(tail == 0, diag, jnp.where(tail == 1, v[:, :HALF], jnp.where(tail == 2, v[:, HALF:], 0.0)))
            out_ref[k, K:, :] = rest.astype(out_ref.dtype)


def local_grams(core, obs_perturb, innovation, error_weight, obs_column, obs_count, radius):
    _, regions, capacity, members = obs_perturb.shape
    smem = pl.BlockSpec(memory_space=pltpu.SMEM)
    vmem = pl.BlockSpec(memory_space=pltpu.VMEM)
    hbm = pl.BlockSpec(memory_space=pltpu.HBM)
    return pl.pallas_call(
        gram_kernel,
        in_specs=[smem] + [hbm] * 6,
        out_specs=[vmem, vmem],
        out_shape=[jax.ShapeDtypeStruct((4, ROWS, HALF), BF16),
                   jax.ShapeDtypeStruct((4, ROWS, HALF), F32)],
        scratch_shapes=[pltpu.VMEM(((regions + 4) * K, K), F32), pltpu.VMEM((regions + 4, K), F32),
                        pltpu.SMEM(obs_count.shape, jnp.int32), pltpu.SMEM(radius.shape, jnp.int32),
                        pltpu.VMEM((regions, capacity, members), BF16),
                        pltpu.VMEM((regions, capacity), F32), pltpu.VMEM((regions, capacity), F32),
                        pltpu.VMEM((regions, capacity), jnp.int32),
                        pltpu.SemaphoreType.DMA((5,)), pltpu.SemaphoreType.DMA((regions,))],
        compiler_params=pltpu.CompilerParams(vmem_limit_bytes=GRAM_VMEM_LIMIT),
        cost_estimate=pl.CostEstimate(flops=10 * regions * capacity * K * K,
                                      bytes_accessed=2 * regions * capacity * K, transcendentals=0),
        name="local_grams",
    )(core, obs_count, radius, obs_perturb, innovation, error_weight, obs_column)


def split_kernel(core_ref, keep_ref, recv_ref, send_ref, mine_ref):
    core = core_ref[0]
    for k in range(3):
        send_ref[k] = (keep_ref[core + k] + recv_ref[core + k].astype(F32)).astype(BF16)
        mine_ref[k] = keep_ref[1 - core + k] + recv_ref[1 - core + k].astype(F32)


def split_sums(core, keep, recv):
    vmem = pl.BlockSpec(memory_space=pltpu.VMEM)
    return pl.pallas_call(
        split_kernel,
        in_specs=[pl.BlockSpec(memory_space=pltpu.SMEM), vmem, vmem],
        out_specs=[vmem, vmem],
        out_shape=[jax.ShapeDtypeStruct((3, ROWS, HALF), BF16),
                   jax.ShapeDtypeStruct((3, ROWS, HALF), F32)],
        compiler_params=pltpu.CompilerParams(vmem_limit_bytes=2 * 1024 * 1024),
        name="split_sums",
    )(core, keep, recv)


def identity_mask(n):
    return lax.broadcasted_iota(jnp.int32, (n, n), 0) == lax.broadcasted_iota(jnp.int32, (n, n), 1)


def product(a, b):
    return jnp.dot(a.astype(BF16), b.astype(BF16), preferred_element_type=F32)


def transform_kernel(mine_ref, halo_ref, other_ref, out_ref):
    row, col = row_col()
    on_diagonal = identity_mask(K)
    count = mine_ref.shape[0]
    state = []
    for k in range(count):
        packed = mine_ref[k] + halo_ref[k].astype(F32) + other_ref[k].astype(F32)
        corner = packed[:HALF]
        both = packed[HALF:K]
        flipped = both.T
        upper = jnp.where(row <= col, both, flipped)
        lower = jnp.where(row > col, both, jnp.where(row == col, packed[K : K + 1], flipped))
        system = jnp.concatenate(
            [jnp.concatenate([upper, corner], axis=1),
             jnp.concatenate([corner.T, lower], axis=1)], axis=0)
        system = system + jnp.where(on_diagonal, (K - 1) / INFLATION, 0.0)
        vec = jnp.concatenate([packed[K + 1 : K + 2], packed[K + 2 : K + 3]], axis=1)
        frob = jnp.sqrt(jnp.sum(jnp.sum(system * system, axis=0, keepdims=True), axis=1, keepdims=True))
        root = system / frob
        rho = jnp.sum(jnp.sum(jnp.where(on_diagonal, root, 0.0), axis=0, keepdims=True), axis=1, keepdims=True) / K
        state.append((root - jnp.where(on_diagonal, rho, 0.0), rho, None, 1.0, frob, vec))
    for iteration in range(NS_ITERS):
        for k in range(count):
            root, rho, inv, iota, frob, vec = state[k]
            mu = 1.5 - 0.5 * iota * rho
            if inv is None:
                mid = -0.5 * root
            else:
                mid = -0.5 * (iota * root + rho * inv + product(inv, root))
            if iteration < NS_ITERS - 1:
                root = rho * mid + mu * root + product(root, mid)
            if inv is None:
                inv = mid
            else:
                inv = mu * inv + iota * mid + product(mid, inv)
            rho, iota = rho * mu, mu * iota
            state[k] = (root, rho, inv, iota, frob, vec)
    for k in range(count):
        _, _, inv, iota, frob, vec = state[k]
        inverse = inv + jnp.where(on_diagonal, iota, 0.0)
        vec_col = jnp.broadcast_to(vec, (HALF, K)).T[:, :1]
        half_step = jnp.sum(inverse * vec_col, axis=0, keepdims=True)
        wbar = jnp.sum(inverse * half_step, axis=1, keepdims=True) / frob
        scale = (K - 1.0) ** 0.5 / jnp.sqrt(frob)
        out_ref[k] = (scale * inverse + wbar).astype(BF16)


def transforms(mine, halo, other):
    vmem = pl.BlockSpec(memory_space=pltpu.VMEM)
    return pl.pallas_call(
        transform_kernel,
        in_specs=[vmem, vmem, vmem],
        out_specs=vmem,
        out_shape=jax.ShapeDtypeStruct((mine.shape[0], K, K), BF16),
        compiler_params=pltpu.CompilerParams(vmem_limit_bytes=VMEM_LIMIT),
        name="transforms",
    )(mine, halo, other)


def update_kernel(core_ref, mine_ref, other_ref, states_ref, out_ref, all_ref):
    region = pl.program_id(0)

    @pl.when(region == 0)
    def _():
        core = core_ref[0]
        all_ref[pl.ds(3 * core, 3)] = mine_ref[...]
        all_ref[pl.ds(3 * (1 - core), 3)] = other_ref[...]

    lags, columns, levels, members = states_ref.shape
    rows = columns * levels // 2
    for lag in range(lags):
        for side in range(2):
            cols = slice(side * columns // 2, (side + 1) * columns // 2)
            state = states_ref[lag, cols].reshape(rows, members).astype(F32)
            mean = jnp.mean(state, axis=1, keepdims=True)
            anomaly = (state - mean).astype(BF16)
            centre = jnp.dot(anomaly, all_ref[region + 1], preferred_element_type=F32)
            beside = jnp.dot(anomaly, all_ref[region + 2 * side], preferred_element_type=F32)
            column = lax.broadcasted_iota(jnp.int32, (rows, 1), 0) // levels + side * columns // 2
            blend = jnp.abs((column.astype(F32) + 0.5) / columns - 0.5)
            result = mean + centre + blend * (beside - centre)
            out_ref[lag, cols] = result.astype(BF16).reshape(columns // 2, levels, members)


def update(core, mine, other, states):
    lags, columns, levels, members = states.shape
    regions = columns // HC
    whole = pl.BlockSpec((3, K, K), lambda r: (0, 0, 0))
    block = pl.BlockSpec((lags, HC, levels, members), lambda r: (0, r, 0, 0))
    return pl.pallas_call(
        update_kernel,
        grid=(regions,),
        in_specs=[pl.BlockSpec(memory_space=pltpu.SMEM), whole, whole, block],
        out_specs=block,
        out_shape=jax.ShapeDtypeStruct(states.shape, BF16),
        scratch_shapes=[pltpu.VMEM((6, K, K), BF16)],
        compiler_params=pltpu.CompilerParams(vmem_limit_bytes=VMEM_LIMIT),
        name="update",
    )(core, mine, other, states)


def shards(obs_perturb, innovation, error_weight, obs_column, obs_count, radius, states):
    core = (lax.axis_index("tm") % 2).astype(jnp.int32).reshape(1)
    spaces = lax.axis_size("space")
    send, keep = local_grams(core, obs_perturb, innovation, error_weight, obs_column, obs_count, radius)
    swap_core = [(0, 1), (1, 0), (2, 3), (3, 2)]
    swap_chip = [(0, 2), (2, 0), (1, 3), (3, 1)]
    recv = lax.ppermute(send, "tm", swap_core)
    edge, mine = split_sums(core, keep, recv)
    perm = []
    for chip in range(2):
        for s in range(spaces):
            low, high = 2 * chip * spaces, (2 * chip + 1) * spaces
            perm.append((high + s, low + (s + 1) % spaces))
            perm.append((low + s, high + (s - 1) % spaces))
    halo = lax.ppermute(edge, ("tm", "space"), perm)
    chip_sum = (mine + halo.astype(F32)).astype(BF16)
    other_chip = lax.ppermute(chip_sum, "tm", swap_chip)
    own = transforms(mine, halo, other_chip)
    beside = lax.ppermute(own, "tm", swap_core)
    return update(core, own, beside, states)


def solution(mesh):
    return jax.shard_map(
        shards,
        mesh=mesh,
        in_specs=(
            P("tm", "space", None, None),
            P("tm", "space", None),
            P("tm", "space", None),
            P("tm", "space", None),
            P("tm", "space"),
            P("space"),
            P("tm", "space", None, None),
        ),
        out_specs=P("tm", "space", None, None),
        check_vma=False,
    )
```

```python
import functools

import jax
import jax.numpy as jnp
from jax import lax
from jax.experimental import pallas as pl
from jax.experimental.pallas import tpu as pltpu
from jax.sharding import PartitionSpec as P

HC = 32
NS_ITERS = 5
INFLATION = 1.1
K = 256
HALF = K // 2
ROWS = HALF + HALF + 16
BF16 = jnp.bfloat16
F32 = jnp.float32
VMEM_LIMIT = 32 * 1024 * 1024


def row_col():
    row = lax.broadcasted_iota(jnp.int32, (HALF, HALF), 0)
    col = lax.broadcasted_iota(jnp.int32, (HALF, HALF), 1)
    return row, col


def tail_row():
    return lax.broadcasted_iota(jnp.int32, (16, HALF), 0)


def observation_weights(innovation, error_weight, obs_column, obs_count, radius):
    _, regions, capacity = innovation.shape
    shape = (regions, 8, capacity)
    offset = lax.broadcasted_iota(jnp.int32, shape, 1).astype(F32) - 2.0
    position = lax.broadcasted_iota(jnp.int32, shape, 2)
    base = jnp.where(position < obs_count[0][:, None, None], error_weight[0][:, None, :], 0.0)
    column = obs_column[0][:, None, :].astype(F32)
    distance = jnp.abs(column + (0.5 - 0.5 * HC) - offset * HC)
    ratio = jnp.minimum(distance / radius[:, None, None].astype(F32), 1.0)
    weight = base * jnp.square(1.0 - ratio * ratio)
    return weight, weight * innovation[0][:, None, :]


def gram_kernel(side_ref, weight_ref, scaled_ref, obs_ref, out_ref, flip_ref):
    side = side_ref[0]
    regions = obs_ref.shape[0]
    row, col = row_col()
    tail = tail_row()
    vecs = []
    for r in range(regions):
        source = r + side * (regions - 1 - 2 * r)
        obs = obs_ref[source]
        flip_ref[r] = obs.T
        scaled = scaled_ref[source]
        high = scaled.astype(BF16)
        low = (scaled - high.astype(F32)).astype(BF16)
        vec = jnp.dot(jnp.concatenate([high, low], axis=0), obs, preferred_element_type=F32)
        vecs.append(vec[:8] + vec[8:])
    for t in reversed(range(regions, 2 * regions)):
        total = None
        vec = None
        for r in reversed(range(regions)):
            m = t - r
            if m > 4:
                continue
            source = r + side * (regions - 1 - 2 * r)
            offset = m + side * (4 - 2 * m)
            weighted = (flip_ref[r].astype(F32) * weight_ref[source, pl.ds(offset, 1), :]).astype(BF16)
            part = jnp.dot(weighted, obs_ref[source], preferred_element_type=F32)
            total = part if total is None else total + part
            part = jnp.where(side == 0, vecs[r][m : m + 1], vecs[r][4 - m : 5 - m])
            vec = part if vec is None else vec + part
        at = t - regions + side * (regions - 1 - 2 * (t - regions))
        out_ref[at, :HALF, :] = total[:HALF, HALF:].astype(out_ref.dtype)
        low = total[HALF:, HALF:]
        out_ref[at, HALF:K, :] = jnp.where(row <= col, total[:HALF, :HALF], low).astype(out_ref.dtype)
        diag = jnp.sum(jnp.where(row == col, low, 0.0), axis=0, keepdims=True)
        rest = jnp.where(tail == 0, diag, jnp.where(tail == 1, vec[:, :HALF], jnp.where(tail == 2, vec[:, HALF:], 0.0)))
        out_ref[at, K:, :] = rest.astype(out_ref.dtype)


def local_grams(side, weight, scaled, obs, dtype, name):
    regions, capacity, members = obs.shape
    vmem = pl.BlockSpec(memory_space=pltpu.VMEM)
    return pl.pallas_call(
        gram_kernel,
        in_specs=[pl.BlockSpec(memory_space=pltpu.SMEM), vmem, vmem, vmem],
        out_specs=vmem,
        out_shape=jax.ShapeDtypeStruct((4, ROWS, HALF), dtype),
        scratch_shapes=[pltpu.VMEM((regions, members, capacity), BF16)],
        compiler_params=pltpu.CompilerParams(vmem_limit_bytes=VMEM_LIMIT),
        cost_estimate=pl.CostEstimate(flops=5 * regions * capacity * K * K,
                                      bytes_accessed=2 * regions * capacity * K, transcendentals=0),
        name=name,
    )(side, weight, scaled, obs)


def split_kernel(core_ref, keep_ref, recv_ref, send_ref, mine_ref):
    core = core_ref[0]
    for k in range(3):
        send_ref[k] = (keep_ref[core + k] + recv_ref[core + k].astype(F32)).astype(BF16)
        mine_ref[k] = keep_ref[1 - core + k] + recv_ref[1 - core + k].astype(F32)


def split_sums(core, keep, recv):
    vmem = pl.BlockSpec(memory_space=pltpu.VMEM)
    return pl.pallas_call(
        split_kernel,
        in_specs=[pl.BlockSpec(memory_space=pltpu.SMEM), vmem, vmem],
        out_specs=[vmem, vmem],
        out_shape=[jax.ShapeDtypeStruct((3, ROWS, HALF), BF16),
                   jax.ShapeDtypeStruct((3, ROWS, HALF), F32)],
        compiler_params=pltpu.CompilerParams(vmem_limit_bytes=2 * 1024 * 1024),
        name="split_sums",
    )(core, keep, recv)


def identity_mask(n):
    return lax.broadcasted_iota(jnp.int32, (n, n), 0) == lax.broadcasted_iota(jnp.int32, (n, n), 1)


def product(a, b):
    return jnp.dot(a.astype(BF16), b.astype(BF16), preferred_element_type=F32)


def transform_kernel(mine_ref, halo_ref, other_ref, out_ref):
    row, col = row_col()
    on_diagonal = identity_mask(K)
    count = mine_ref.shape[0]
    state = []
    for k in range(count):
        packed = mine_ref[k] + halo_ref[k].astype(F32) + other_ref[k].astype(F32)
        corner = packed[:HALF]
        both = packed[HALF:K]
        flipped = both.T
        upper = jnp.where(row <= col, both, flipped)
        lower = jnp.where(row > col, both, jnp.where(row == col, packed[K : K + 1], flipped))
        system = jnp.concatenate(
            [jnp.concatenate([upper, corner], axis=1),
             jnp.concatenate([corner.T, lower], axis=1)], axis=0)
        system = system + jnp.where(on_diagonal, (K - 1) / INFLATION, 0.0)
        vec = jnp.concatenate([packed[K + 1 : K + 2], packed[K + 2 : K + 3]], axis=1)
        frob = jnp.sqrt(jnp.sum(jnp.sum(system * system, axis=0, keepdims=True), axis=1, keepdims=True))
        shrink = 1.0 / frob
        trace = jnp.sum(jnp.sum(jnp.where(on_diagonal, system, 0.0), axis=0, keepdims=True), axis=1, keepdims=True)
        root = system * shrink
        rho = trace * shrink * (1.0 / K)
        state.append((root - jnp.where(on_diagonal, rho, 0.0), rho, None, 1.0, frob, vec))
    for iteration in range(NS_ITERS):
        for k in range(count):
            root, rho, inv, iota, frob, vec = state[k]
            mu = 1.5 - 0.5 * iota * rho
            if inv is None:
                mid = -0.5 * root
            else:
                mid = -0.5 * (iota * root + rho * inv + product(inv, root))
            if iteration < NS_ITERS - 1:
                root = rho * mid + mu * root + product(root, mid)
            if inv is None:
                inv = mid
            else:
                inv = mu * inv + iota * mid + product(mid, inv)
            rho, iota = rho * mu, mu * iota
            state[k] = (root, rho, inv, iota, frob, vec)
    for k in range(count):
        _, _, inv, iota, frob, vec = state[k]
        inverse = inv + jnp.where(on_diagonal, iota, 0.0)
        vec_col = jnp.broadcast_to(vec, (HALF, K)).T[:, :1]
        half_step = jnp.sum(inverse * vec_col, axis=0, keepdims=True)
        wbar = jnp.sum(inverse * half_step, axis=1, keepdims=True) / frob
        scale = (K - 1.0) ** 0.5 / jnp.sqrt(frob)
        out_ref[k] = (scale * inverse + wbar).astype(BF16)


def transforms(mine, halo, other):
    vmem = pl.BlockSpec(memory_space=pltpu.VMEM)
    return pl.pallas_call(
        transform_kernel,
        in_specs=[vmem, vmem, vmem],
        out_specs=vmem,
        out_shape=jax.ShapeDtypeStruct((mine.shape[0], K, K), BF16),
        compiler_params=pltpu.CompilerParams(vmem_limit_bytes=VMEM_LIMIT),
        name="transforms",
    )(mine, halo, other)


def anomaly_kernel(states_ref, anomaly_ref, mean_ref):
    lags, columns, levels, members = states_ref.shape
    rows = lags * columns * levels
    state = states_ref[...].reshape(rows, members).astype(F32)
    mean = jnp.mean(state, axis=1, keepdims=True)
    anomaly_ref[...] = (state - mean).astype(BF16).reshape(states_ref.shape)
    mean_ref[...] = jnp.broadcast_to(mean, (rows, HALF)).reshape(mean_ref.shape)


def anomalies(states):
    lags, columns, levels, members = states.shape
    block = pl.BlockSpec((lags, HC, levels, members), lambda r: (0, r, 0, 0))
    mean_block = pl.BlockSpec((lags, HC, levels, HALF), lambda r: (0, r, 0, 0))
    return pl.pallas_call(
        anomaly_kernel,
        grid=(columns // HC,),
        in_specs=[block],
        out_specs=[block, mean_block],
        out_shape=[jax.ShapeDtypeStruct(states.shape, BF16),
                   jax.ShapeDtypeStruct(states.shape[:-1] + (HALF,), F32)],
        compiler_params=pltpu.CompilerParams(vmem_limit_bytes=VMEM_LIMIT),
        cost_estimate=pl.CostEstimate(flops=4 * states.size, bytes_accessed=8 * states.size, transcendentals=0),
        name="anomalies",
    )(states)


def update_block(anomaly_ref, mean_ref, out_ref, centre_t, side_t):
    lags, columns, levels, members = anomaly_ref.shape
    half = columns // 2
    rows = half * levels
    for lag in range(lags):
        for side in range(2):
            cols = slice(side * half, (side + 1) * half)
            anomaly = anomaly_ref[lag, cols].reshape(rows, members)
            centre = jnp.dot(anomaly, centre_t, preferred_element_type=F32)
            beside = jnp.dot(anomaly, side_t(side), preferred_element_type=F32)
            column = lax.broadcasted_iota(jnp.int32, (half, levels, members), 0) + side * half
            blend = jnp.abs((column.astype(F32) + 0.5) / columns - 0.5).reshape(rows, members)
            mean = mean_ref[lag, cols].reshape(rows, HALF)
            result = jnp.concatenate([mean, mean], axis=1) + (centre + blend * (beside - centre))
            out_ref[lag, cols] = result.astype(BF16).reshape(half, levels, members)


def first_update_kernel(core_ref, mine_ref, anomaly_ref, mean_ref, out_ref):
    update_block(anomaly_ref, mean_ref, out_ref, mine_ref[1], lambda side: mine_ref[2 * side])


def last_update_kernel(core_ref, mine_ref, other_ref, anomaly_ref, mean_ref, _, out_ref, all_ref):
    step = pl.program_id(0)
    core = core_ref[0]

    @pl.when(step == 0)
    def _():
        all_ref[pl.ds(3 * core, 3)] = mine_ref[...]
        all_ref[pl.ds(3 * (1 - core), 3)] = other_ref[...]

    region = step + 1 - core
    update_block(anomaly_ref, mean_ref, out_ref, all_ref[region + 1], lambda side: all_ref[region + 2 * side])


def update_specs(shape, region_of, transforms_taken):
    lags, columns, levels, members = shape
    whole = pl.BlockSpec((3, K, K), lambda r, core: (0, 0, 0))
    block = pl.BlockSpec((lags, HC, levels, members), lambda r, core: (0, region_of(r, core), 0, 0))
    mean_block = pl.BlockSpec((lags, HC, levels, HALF), lambda r, core: (0, region_of(r, core), 0, 0))
    return [whole] * transforms_taken + [block, mean_block], block


def first_update(core, mine, anomaly, mean):
    regions = anomaly.shape[1] // HC
    in_specs, block = update_specs(anomaly.shape, lambda r, core: core[0] * (regions - 1), 1)
    return pl.pallas_call(
        first_update_kernel,
        grid_spec=pltpu.PrefetchScalarGridSpec(
            num_scalar_prefetch=1, grid=(1,), in_specs=in_specs, out_specs=block),
        out_shape=jax.ShapeDtypeStruct(anomaly.shape, BF16),
        compiler_params=pltpu.CompilerParams(vmem_limit_bytes=VMEM_LIMIT),
        cost_estimate=pl.CostEstimate(flops=anomaly.size * K, bytes_accessed=anomaly.size, transcendentals=0),
        name="first_update",
    )(core, mine, anomaly, mean)


def last_update(core, mine, other, anomaly, mean, begun):
    regions = anomaly.shape[1] // HC
    in_specs, block = update_specs(anomaly.shape, lambda r, core: r + 1 - core[0], 2)
    return pl.pallas_call(
        last_update_kernel,
        grid_spec=pltpu.PrefetchScalarGridSpec(
            num_scalar_prefetch=1, grid=(regions - 1,),
            in_specs=in_specs + [pl.BlockSpec(memory_space=pl.ANY)], out_specs=block,
            scratch_shapes=[pltpu.VMEM((6, K, K), BF16)]),
        out_shape=jax.ShapeDtypeStruct(anomaly.shape, BF16),
        input_output_aliases={5: 0},
        compiler_params=pltpu.CompilerParams(vmem_limit_bytes=VMEM_LIMIT),
        cost_estimate=pl.CostEstimate(flops=3 * anomaly.size * K, bytes_accessed=3 * anomaly.size, transcendentals=0),
        name="last_update",
    )(core, mine, other, anomaly, mean, begun)


def shards(obs_perturb, innovation, error_weight, obs_column, obs_count, radius, states):
    core = (lax.axis_index("tm") % 2).astype(jnp.int32).reshape(1)
    spaces = lax.axis_size("space")
    weight, scaled = observation_weights(innovation, error_weight, obs_column, obs_count, radius)
    send = local_grams(core, weight, scaled, obs_perturb[0], BF16, "grams_to_send")
    keep = local_grams(1 - core, weight, scaled, obs_perturb[0], F32, "grams_to_keep")
    swap_core = [(0, 1), (1, 0), (2, 3), (3, 2)]
    swap_chip = [(0, 2), (2, 0), (1, 3), (3, 1)]
    recv = lax.ppermute(send, "tm", swap_core)
    edge, mine = split_sums(core, keep, recv)
    perm = []
    for chip in range(2):
        for s in range(spaces):
            low, high = 2 * chip * spaces, (2 * chip + 1) * spaces
            perm.append((high + s, low + (s + 1) % spaces))
            perm.append((low + s, high + (s - 1) % spaces))
    states, edge = lax.optimization_barrier((states, edge))
    halo = lax.ppermute(edge, ("tm", "space"), perm)
    halo, anomaly, mean = lax.optimization_barrier((halo, *anomalies(states)))
    chip_sum = (mine + halo.astype(F32)).astype(BF16)
    other_chip = lax.ppermute(chip_sum, "tm", swap_chip)
    own = transforms(mine, halo, other_chip)
    beside = lax.ppermute(own, "tm", swap_core)
    begun = first_update(core, own, anomaly, mean)
    return last_update(core, own, beside, anomaly, mean, begun)


def solution(mesh):
    return jax.shard_map(
        shards,
        mesh=mesh,
        in_specs=(
            P("tm", "space", None, None),
            P("tm", "space", None),
            P("tm", "space", None),
            P("tm", "space", None),
            P("tm", "space"),
            P("space"),
            P("tm", "space", None, None),
        ),
        out_specs=P("tm", "space", None, None),
        check_vma=False,
    )
```

```python
import functools

import jax
import jax.numpy as jnp
from jax import lax
from jax.experimental import pallas as pl
from jax.experimental.pallas import tpu as pltpu
from jax.sharding import PartitionSpec as P

HC = 32
NS_ITERS = 5
INFLATION = 1.1
K = 256
HALF = K // 2
ROWS = HALF + HALF + 16
BF16 = jnp.bfloat16
F32 = jnp.float32
VMEM_LIMIT = 32 * 1024 * 1024


def row_col():
    row = lax.broadcasted_iota(jnp.int32, (HALF, HALF), 0)
    col = lax.broadcasted_iota(jnp.int32, (HALF, HALF), 1)
    return row, col


def tail_row():
    return lax.broadcasted_iota(jnp.int32, (16, HALF), 0)


def observation_weights(innovation, error_weight, obs_column, obs_count, radius):
    _, regions, capacity = innovation.shape
    position = lax.broadcasted_iota(jnp.int32, (regions, capacity), 1)
    base = jnp.where(position < obs_count[0][:, None], error_weight[0], 0.0)
    place = obs_column[0].astype(F32) + (0.5 - 0.5 * HC)
    reach = radius.astype(F32)[:, None]
    offset = lax.broadcasted_iota(jnp.int32, (5, regions, capacity), 0).astype(F32) - 2.0
    ratio = jnp.minimum(jnp.abs(place[None] - offset * HC) / reach[None], 1.0)
    weight = base[None] * jnp.square(1.0 - ratio * ratio)
    return weight, weight * innovation[0][None]


def gram_kernel(side_ref, weight_ref, scaled_ref, obs_ref, out_ref, flip_ref):
    side = side_ref[0]
    regions = obs_ref.shape[0]
    row, col = row_col()
    tail = tail_row()
    vecs = []
    for r in range(regions):
        source = r + side * (regions - 1 - 2 * r)
        obs = obs_ref[source]
        flip_ref[r] = obs.T
        here = pl.ds(source, 1)
        scaled = jnp.concatenate([scaled_ref[m, here, :] for m in (0, 1, 2, 3, 4, 4, 4, 4)], axis=0)
        high = scaled.astype(BF16)
        low = (scaled - high.astype(F32)).astype(BF16)
        vec = jnp.dot(jnp.concatenate([high, low], axis=0), obs, preferred_element_type=F32)
        vecs.append(vec[:8] + vec[8:])
    for t in reversed(range(regions, 2 * regions)):
        total = None
        vec = None
        for r in reversed(range(regions)):
            m = t - r
            if m > 4:
                continue
            source = r + side * (regions - 1 - 2 * r)
            offset = m + side * (4 - 2 * m)
            weighted = (flip_ref[r].astype(F32) * weight_ref[offset, pl.ds(source, 1), :]).astype(BF16)
            part = jnp.dot(weighted, obs_ref[source], preferred_element_type=F32)
            total = part if total is None else total + part
            part = jnp.where(side == 0, vecs[r][m : m + 1], vecs[r][4 - m : 5 - m])
            vec = part if vec is None else vec + part
        at = t - regions + side * (regions - 1 - 2 * (t - regions))
        out_ref[at, :HALF, :] = total[:HALF, HALF:].astype(out_ref.dtype)
        low = total[HALF:, HALF:]
        out_ref[at, HALF:K, :] = jnp.where(row <= col, total[:HALF, :HALF], low).astype(out_ref.dtype)
        diag = jnp.sum(jnp.where(row == col, low, 0.0), axis=0, keepdims=True)
        rest = jnp.where(tail == 0, diag, jnp.where(tail == 1, vec[:, :HALF], jnp.where(tail == 2, vec[:, HALF:], 0.0)))
        out_ref[at, K:, :] = rest.astype(out_ref.dtype)


def local_grams(side, weight, scaled, obs, dtype, name):
    regions, capacity, members = obs.shape
    vmem = pl.BlockSpec(memory_space=pltpu.VMEM)
    return pl.pallas_call(
        gram_kernel,
        in_specs=[pl.BlockSpec(memory_space=pltpu.SMEM), vmem, vmem, vmem],
        out_specs=vmem,
        out_shape=jax.ShapeDtypeStruct((4, ROWS, HALF), dtype),
        scratch_shapes=[pltpu.VMEM((regions, members, capacity), BF16)],
        compiler_params=pltpu.CompilerParams(vmem_limit_bytes=VMEM_LIMIT),
        cost_estimate=pl.CostEstimate(flops=5 * regions * capacity * K * K,
                                      bytes_accessed=2 * regions * capacity * K, transcendentals=0),
        name=name,
    )(side, weight, scaled, obs)


def split_kernel(core_ref, keep_ref, recv_ref, send_ref, mine_ref):
    core = core_ref[0]
    for k in range(3):
        send_ref[k] = (keep_ref[core + k] + recv_ref[core + k].astype(F32)).astype(BF16)
        mine_ref[k] = keep_ref[1 - core + k] + recv_ref[1 - core + k].astype(F32)


def split_sums(core, keep, recv):
    vmem = pl.BlockSpec(memory_space=pltpu.VMEM)
    return pl.pallas_call(
        split_kernel,
        in_specs=[pl.BlockSpec(memory_space=pltpu.SMEM), vmem, vmem],
        out_specs=[vmem, vmem],
        out_shape=[jax.ShapeDtypeStruct((3, ROWS, HALF), BF16),
                   jax.ShapeDtypeStruct((3, ROWS, HALF), F32)],
        compiler_params=pltpu.CompilerParams(vmem_limit_bytes=2 * 1024 * 1024),
        name="split_sums",
    )(core, keep, recv)


def identity_mask(n):
    return lax.broadcasted_iota(jnp.int32, (n, n), 0) == lax.broadcasted_iota(jnp.int32, (n, n), 1)


def product(a, b):
    return jnp.dot(a.astype(BF16), b.astype(BF16), preferred_element_type=F32)


def transform_kernel(mine_ref, halo_ref, other_ref, out_ref):
    row, col = row_col()
    on_diagonal = identity_mask(K)
    count = mine_ref.shape[0]
    state = []
    for k in range(count):
        packed = mine_ref[k] + halo_ref[k].astype(F32) + other_ref[k].astype(F32)
        corner = packed[:HALF]
        both = packed[HALF:K]
        flipped = both.T
        upper = jnp.where(row <= col, both, flipped)
        lower = jnp.where(row > col, both, jnp.where(row == col, packed[K : K + 1], flipped))
        system = jnp.concatenate(
            [jnp.concatenate([upper, corner], axis=1),
             jnp.concatenate([corner.T, lower], axis=1)], axis=0)
        system = system + jnp.where(on_diagonal, (K - 1) / INFLATION, 0.0)
        vec = jnp.concatenate([packed[K + 1 : K + 2], packed[K + 2 : K + 3]], axis=1)
        frob = jnp.sqrt(jnp.sum(jnp.sum(system * system, axis=0, keepdims=True), axis=1, keepdims=True))
        shrink = 1.0 / frob
        trace = jnp.sum(jnp.sum(jnp.where(on_diagonal, system, 0.0), axis=0, keepdims=True), axis=1, keepdims=True)
        root = system * shrink
        rho = trace * shrink * (1.0 / K)
        state.append((root - jnp.where(on_diagonal, rho, 0.0), rho, None, 1.0, frob, vec))
    for iteration in range(NS_ITERS):
        last = iteration == NS_ITERS - 1
        halves = [state[k][0].astype(BF16) for k in range(count)]
        squares, crosses = [], []
        for k in range(count):
            inv = state[k][2]
            squares.append(None if last else product(halves[k], halves[k]))
            crosses.append(None if inv is None else product(inv, halves[k]))
        for k in range(count):
            w, y, inv, iota, frob, vec = state[k]
            mu = 1.5 - 0.5 * y
            inv = -0.5 * w if inv is None else mu * inv - (0.5 * iota) * w - 0.5 * crosses[k]
            if not last:
                square = squares[k]
                w = (mu * (1.5 - 1.5 * y)) * w + (0.75 * y - 1.5) * square + 0.25 * product(halves[k], square)
            state[k] = (w, y * mu * mu, inv, iota * mu, frob, vec)
    for k in range(count):
        _, _, inv, iota, frob, vec = state[k]
        inverse = inv + jnp.where(on_diagonal, iota, 0.0)
        vec_col = jnp.broadcast_to(vec, (HALF, K)).T[:, :1]
        half_step = jnp.sum(inverse * vec_col, axis=0, keepdims=True)
        wbar = jnp.sum(inverse * half_step, axis=1, keepdims=True) / frob
        scale = (K - 1.0) ** 0.5 / jnp.sqrt(frob)
        out_ref[k] = (scale * inverse + wbar).astype(BF16)


def transforms(mine, halo, other):
    vmem = pl.BlockSpec(memory_space=pltpu.VMEM)
    return pl.pallas_call(
        transform_kernel,
        in_specs=[vmem, vmem, vmem],
        out_specs=vmem,
        out_shape=jax.ShapeDtypeStruct((mine.shape[0], K, K), BF16),
        compiler_params=pltpu.CompilerParams(vmem_limit_bytes=VMEM_LIMIT),
        name="transforms",
    )(mine, halo, other)


def anomaly_kernel(states_ref, pair_ref, mean_ref):
    lags, columns, levels, members = states_ref.shape
    rows = lags * columns * levels
    state = states_ref[...].reshape(rows, members).astype(F32)
    mean = jnp.mean(state, axis=1, keepdims=True)
    anomaly = (state - mean).astype(BF16).reshape(states_ref.shape)
    column = lax.broadcasted_iota(jnp.int32, states_ref.shape, 1)
    blend = jnp.abs((column.astype(F32) + 0.5) / columns - 0.5)
    pair_ref[:, :, :, :members] = anomaly
    pair_ref[:, :, :, members:] = (anomaly.astype(F32) * blend).astype(BF16)
    mean_ref[...] = jnp.broadcast_to(mean, (rows, HALF)).reshape(mean_ref.shape)


def anomalies(states):
    lags, columns, levels, members = states.shape
    block = lambda width: pl.BlockSpec((lags, HC, levels, width), lambda r: (0, r, 0, 0))
    return pl.pallas_call(
        anomaly_kernel,
        grid=(columns // HC,),
        in_specs=[block(members)],
        out_specs=[block(2 * members), block(HALF)],
        out_shape=[jax.ShapeDtypeStruct(states.shape[:-1] + (2 * members,), BF16),
                   jax.ShapeDtypeStruct(states.shape[:-1] + (HALF,), F32)],
        compiler_params=pltpu.CompilerParams(vmem_limit_bytes=VMEM_LIMIT),
        cost_estimate=pl.CostEstimate(flops=4 * states.size, bytes_accessed=8 * states.size, transcendentals=0),
        name="anomalies",
    )(states)


def update_region(region, slot, transform_of, pair_ref, mean_ref, out_ref, done_ref, sems):
    lags, _, levels, members = out_ref.shape
    half = HC // 2
    rows = half * levels
    centre = transform_of(1)
    stacked = []
    for side in range(2):
        change = transform_of(2 * side).astype(F32) - centre.astype(F32)
        stacked.append(jnp.concatenate([centre, change.astype(BF16)], axis=0))
    copies = []
    for lag in range(lags):
        for side in range(2):
            cols = pl.ds(region * HC + side * half, half)
            pair = pair_ref[lag, cols].reshape(rows, 2 * members)
            moved = jnp.dot(pair, stacked[side], preferred_element_type=F32)
            mean = mean_ref[lag, cols].reshape(rows, HALF)
            result = jnp.concatenate([mean, mean], axis=1) + moved
            done_ref[slot, lag, side * half : (side + 1) * half] = result.astype(BF16).reshape(half, levels, members)
        copy = pltpu.make_async_copy(
            done_ref.at[slot, lag], out_ref.at[lag, pl.ds(region * HC, HC)], sems.at[slot, lag])
        copy.start()
        copies.append(copy)
    return copies


def first_update_kernel(core_ref, mine_ref, pair_ref, mean_ref, out_ref, done_ref, sems):
    region = core_ref[0] * (pair_ref.shape[1] // HC - 1)
    for copy in update_region(region, 0, lambda k: mine_ref[k], pair_ref, mean_ref, out_ref, done_ref, sems):
        copy.wait()


def last_update_kernel(core_ref, mine_ref, other_ref, pair_ref, mean_ref, _, out_ref, all_ref, done_ref, sems):
    core = core_ref[0]
    all_ref[pl.ds(3 * core, 3)] = mine_ref[...]
    all_ref[pl.ds(3 * (1 - core), 3)] = other_ref[...]
    copies = []
    for step in range(done_ref.shape[0]):
        region = step + 1 - core
        copies += update_region(region, step, lambda k: all_ref[region + k], pair_ref, mean_ref, out_ref, done_ref, sems)
    for copy in copies:
        copy.wait()


def update_call(kernel, args, begun, states, count, scratch, name):
    lags, columns, levels, members = states.shape
    vmem = pl.BlockSpec(memory_space=pltpu.VMEM)
    given = [] if begun is None else [begun]
    flops = 2 * count * lags * HC * levels * 2 * members * members
    return pl.pallas_call(
        kernel,
        in_specs=[pl.BlockSpec(memory_space=pltpu.SMEM)] + [vmem] * (len(args) - 1) + [pl.BlockSpec(memory_space=pl.ANY)] * len(given),
        out_specs=pl.BlockSpec(memory_space=pl.ANY),
        out_shape=jax.ShapeDtypeStruct(states.shape, BF16),
        scratch_shapes=scratch + [pltpu.VMEM((count, lags, HC, levels, members), BF16),
                                  pltpu.SemaphoreType.DMA((count, lags))],
        input_output_aliases={len(args): 0} if given else {},
        compiler_params=pltpu.CompilerParams(vmem_limit_bytes=VMEM_LIMIT),
        cost_estimate=pl.CostEstimate(flops=flops, bytes_accessed=count * lags * HC * levels * members * 6, transcendentals=0),
        name=name,
    )(*args, *given)


def first_update(core, mine, pair, mean, states):
    return update_call(first_update_kernel, (core, mine, pair, mean), None, states, 1, [], "first_update")


def last_update(core, mine, other, pair, mean, begun):
    count = begun.shape[1] // HC - 1
    return update_call(last_update_kernel, (core, mine, other, pair, mean), begun, begun, count,
                       [pltpu.VMEM((6, K, K), BF16)], "last_update")


def shards(obs_perturb, innovation, error_weight, obs_column, obs_count, radius, states):
    core = (lax.axis_index("tm") % 2).astype(jnp.int32).reshape(1)
    spaces = lax.axis_size("space")
    weight, scaled = observation_weights(innovation, error_weight, obs_column, obs_count, radius)
    send = local_grams(core, weight, scaled, obs_perturb[0], BF16, "grams_to_send")
    keep = local_grams(1 - core, weight, scaled, obs_perturb[0], F32, "grams_to_keep")
    swap_core = [(0, 1), (1, 0), (2, 3), (3, 2)]
    swap_chip = [(0, 2), (2, 0), (1, 3), (3, 1)]
    recv = lax.ppermute(send, "tm", swap_core)
    edge, mine = split_sums(core, keep, recv)
    perm = []
    for chip in range(2):
        for s in range(spaces):
            low, high = 2 * chip * spaces, (2 * chip + 1) * spaces
            perm.append((high + s, low + (s + 1) % spaces))
            perm.append((low + s, high + (s - 1) % spaces))
    states, edge = lax.optimization_barrier((states, edge))
    halo = lax.ppermute(edge, ("tm", "space"), perm)
    halo, pair, mean = lax.optimization_barrier((halo, *anomalies(states)))
    chip_sum = (mine + halo.astype(F32)).astype(BF16)
    other_chip = lax.ppermute(chip_sum, "tm", swap_chip)
    own = transforms(mine, halo, other_chip)
    beside = lax.ppermute(own, "tm", swap_core)
    begun = first_update(core, own, pair, mean, states)
    return last_update(core, own, beside, pair, mean, begun)


def solution(mesh):
    return jax.shard_map(
        shards,
        mesh=mesh,
        in_specs=(
            P("tm", "space", None, None),
            P("tm", "space", None),
            P("tm", "space", None),
            P("tm", "space", None),
            P("tm", "space"),
            P("space"),
            P("tm", "space", None, None),
        ),
        out_specs=P("tm", "space", None, None),
        check_vma=False,
    )
```

```python
import functools

import jax
import jax.numpy as jnp
from jax import lax
from jax.experimental import pallas as pl
from jax.experimental.pallas import tpu as pltpu
from jax.sharding import PartitionSpec as P

HC = 32
NS_ITERS = 5
INFLATION = 1.1
K = 256
HALF = K // 2
ROWS = HALF + HALF + 16
BF16 = jnp.bfloat16
F32 = jnp.float32
VMEM_LIMIT = 32 * 1024 * 1024


def row_col():
    row = lax.broadcasted_iota(jnp.int32, (HALF, HALF), 0)
    col = lax.broadcasted_iota(jnp.int32, (HALF, HALF), 1)
    return row, col


def tail_row():
    return lax.broadcasted_iota(jnp.int32, (16, HALF), 0)


def observation_terms(innovation, error_weight, obs_column, obs_count, radius):
    column = obs_column[0]
    position = lax.broadcasted_iota(jnp.int32, column.shape, 1)
    base = jnp.where(position < obs_count[0][:, None], error_weight[0], 0.0)
    reach = jnp.maximum(radius[:, None], column).astype(F32)
    return base, base * innovation[0], (column.astype(F32) + (0.5 - 0.5 * HC)) / reach, HC / reach


def gram_kernel(side_ref, base_ref, innov_ref, place_ref, width_ref, obs_ref, out_ref, flip_ref, weight_ref, scaled_ref):
    side = side_ref[0]
    regions = obs_ref.shape[0]
    for m in range(5):
        ratio = jnp.minimum(jnp.abs(place_ref[...] - (m - 2.0) * width_ref[...]), 1.0)
        taper = jnp.square(1.0 - ratio * ratio)
        weight_ref[m] = base_ref[...] * taper
        scaled_ref[m] = innov_ref[...] * taper
    row, col = row_col()
    tail = tail_row()
    vecs = []
    for r in range(regions):
        source = r + side * (regions - 1 - 2 * r)
        obs = obs_ref[source]
        flip_ref[r] = obs.T
        here = pl.ds(source, 1)
        scaled = jnp.concatenate([scaled_ref[m, here, :] for m in (0, 1, 2, 3, 4, 4, 4, 4)], axis=0)
        high = scaled.astype(BF16)
        low = (scaled - high.astype(F32)).astype(BF16)
        vec = jnp.dot(jnp.concatenate([high, low], axis=0), obs, preferred_element_type=F32)
        vecs.append(vec[:8] + vec[8:])
    for t in reversed(range(regions, 2 * regions)):
        total = None
        vec = None
        for r in reversed(range(regions)):
            m = t - r
            if m > 4:
                continue
            source = r + side * (regions - 1 - 2 * r)
            offset = m + side * (4 - 2 * m)
            weighted = (flip_ref[r].astype(F32) * weight_ref[offset, pl.ds(source, 1), :]).astype(BF16)
            part = jnp.dot(weighted, obs_ref[source], preferred_element_type=F32)
            total = part if total is None else total + part
            part = jnp.where(side == 0, vecs[r][m : m + 1], vecs[r][4 - m : 5 - m])
            vec = part if vec is None else vec + part
        at = t - regions + side * (regions - 1 - 2 * (t - regions))
        out_ref[at, :HALF, :] = total[:HALF, HALF:].astype(out_ref.dtype)
        low = total[HALF:, HALF:]
        out_ref[at, HALF:K, :] = jnp.where(row <= col, total[:HALF, :HALF], low).astype(out_ref.dtype)
        diag = jnp.sum(jnp.where(row == col, low, 0.0), axis=0, keepdims=True)
        rest = jnp.where(tail == 0, diag, jnp.where(tail == 1, vec[:, :HALF], jnp.where(tail == 2, vec[:, HALF:], 0.0)))
        out_ref[at, K:, :] = rest.astype(out_ref.dtype)


def local_grams(side, terms, obs, dtype, name):
    regions, capacity, members = obs.shape
    vmem = pl.BlockSpec(memory_space=pltpu.VMEM)
    return pl.pallas_call(
        gram_kernel,
        in_specs=[pl.BlockSpec(memory_space=pltpu.SMEM)] + [vmem] * 5,
        out_specs=vmem,
        out_shape=jax.ShapeDtypeStruct((4, ROWS, HALF), dtype),
        scratch_shapes=[pltpu.VMEM((regions, members, capacity), BF16)] + [pltpu.VMEM((5, regions, capacity), F32)] * 2,
        compiler_params=pltpu.CompilerParams(vmem_limit_bytes=VMEM_LIMIT),
        cost_estimate=pl.CostEstimate(flops=5 * regions * capacity * K * K,
                                      bytes_accessed=2 * regions * capacity * K, transcendentals=0),
        name=name,
    )(side, *terms, obs)


def split_kernel(core_ref, keep_ref, recv_ref, send_ref, mine_ref):
    core = core_ref[0]
    for k in range(3):
        send_ref[k] = (keep_ref[core + k] + recv_ref[core + k].astype(F32)).astype(BF16)
        mine_ref[k] = keep_ref[1 - core + k] + recv_ref[1 - core + k].astype(F32)


def split_sums(core, keep, recv):
    vmem = pl.BlockSpec(memory_space=pltpu.VMEM)
    return pl.pallas_call(
        split_kernel,
        in_specs=[pl.BlockSpec(memory_space=pltpu.SMEM), vmem, vmem],
        out_specs=[vmem, vmem],
        out_shape=[jax.ShapeDtypeStruct((3, ROWS, HALF), BF16),
                   jax.ShapeDtypeStruct((3, ROWS, HALF), F32)],
        compiler_params=pltpu.CompilerParams(vmem_limit_bytes=2 * 1024 * 1024),
        name="split_sums",
    )(core, keep, recv)


def identity_mask(n):
    return lax.broadcasted_iota(jnp.int32, (n, n), 0) == lax.broadcasted_iota(jnp.int32, (n, n), 1)


def product(a, b):
    return jnp.dot(a.astype(BF16), b.astype(BF16), preferred_element_type=F32)


def transform_kernel(mine_ref, halo_ref, other_ref, out_ref):
    row, col = row_col()
    on_diagonal = identity_mask(K)
    count = mine_ref.shape[0]
    state = []
    for k in range(count):
        packed = mine_ref[k] + halo_ref[k].astype(F32) + other_ref[k].astype(F32)
        corner = packed[:HALF]
        both = packed[HALF:K]
        flipped = both.T
        upper = jnp.where(row <= col, both, flipped)
        lower = jnp.where(row > col, both, jnp.where(row == col, packed[K : K + 1], flipped))
        system = jnp.concatenate(
            [jnp.concatenate([upper, corner], axis=1),
             jnp.concatenate([corner.T, lower], axis=1)], axis=0)
        system = system + jnp.where(on_diagonal, (K - 1) / INFLATION, 0.0)
        vec = jnp.concatenate([packed[K + 1 : K + 2], packed[K + 2 : K + 3]], axis=1)
        frob = jnp.sqrt(jnp.sum(jnp.sum(system * system, axis=0, keepdims=True), axis=1, keepdims=True))
        shrink = 1.0 / frob
        trace = jnp.sum(jnp.sum(jnp.where(on_diagonal, system, 0.0), axis=0, keepdims=True), axis=1, keepdims=True)
        root = system * shrink
        rho = trace * shrink * (1.0 / K)
        state.append((root - jnp.where(on_diagonal, rho, 0.0), rho, None, 1.0, frob, vec))
    for iteration in range(NS_ITERS):
        last = iteration == NS_ITERS - 1
        halves = [state[k][0].astype(BF16) for k in range(count)]
        squares, crosses = [], []
        for k in range(count):
            inv = state[k][2]
            squares.append(None if last else product(halves[k], halves[k]))
            crosses.append(None if inv is None else product(inv, halves[k]))
        for k in range(count):
            w, y, inv, iota, frob, vec = state[k]
            mu = 1.5 - 0.5 * y
            inv = -0.5 * w if inv is None else mu * inv - (0.5 * iota) * w - 0.5 * crosses[k]
            if not last:
                square = squares[k]
                w = (mu * (1.5 - 1.5 * y)) * w + (0.75 * y - 1.5) * square + 0.25 * product(halves[k], square)
            state[k] = (w, y * mu * mu, inv, iota * mu, frob, vec)
    for k in range(count):
        _, _, inv, iota, frob, vec = state[k]
        inverse = inv + jnp.where(on_diagonal, iota, 0.0)
        vec_col = jnp.broadcast_to(vec, (HALF, K)).T[:, :1]
        half_step = jnp.sum(inverse * vec_col, axis=0, keepdims=True)
        wbar = jnp.sum(inverse * half_step, axis=1, keepdims=True) / frob
        scale = (K - 1.0) ** 0.5 / jnp.sqrt(frob)
        out_ref[k] = (scale * inverse + wbar).astype(BF16)


def transforms(mine, halo, other):
    vmem = pl.BlockSpec(memory_space=pltpu.VMEM)
    return pl.pallas_call(
        transform_kernel,
        in_specs=[vmem, vmem, vmem],
        out_specs=vmem,
        out_shape=jax.ShapeDtypeStruct((mine.shape[0], K, K), BF16),
        compiler_params=pltpu.CompilerParams(vmem_limit_bytes=VMEM_LIMIT),
        name="transforms",
    )(mine, halo, other)


def anomaly_kernel(states_ref, pair_ref, mean_ref):
    lags, columns, levels, members = states_ref.shape
    rows = lags * columns * levels
    state = states_ref[...].reshape(rows, members).astype(F32)
    mean = jnp.mean(state, axis=1, keepdims=True)
    anomaly = (state - mean).astype(BF16).reshape(states_ref.shape)
    column = lax.broadcasted_iota(jnp.int32, states_ref.shape, 1)
    blend = jnp.abs((column.astype(F32) + 0.5) / columns - 0.5)
    pair_ref[:, :, :, :members] = anomaly
    pair_ref[:, :, :, members:] = (anomaly.astype(F32) * blend).astype(BF16)
    mean_ref[...] = jnp.broadcast_to(mean, (rows, HALF)).reshape(mean_ref.shape)


def anomalies(states):
    lags, columns, levels, members = states.shape
    block = lambda width: pl.BlockSpec((lags, HC, levels, width), lambda r: (0, r, 0, 0))
    return pl.pallas_call(
        anomaly_kernel,
        grid=(columns // HC,),
        in_specs=[block(members)],
        out_specs=[block(2 * members), block(HALF)],
        out_shape=[jax.ShapeDtypeStruct(states.shape[:-1] + (2 * members,), BF16),
                   jax.ShapeDtypeStruct(states.shape[:-1] + (HALF,), F32)],
        compiler_params=pltpu.CompilerParams(vmem_limit_bytes=VMEM_LIMIT),
        cost_estimate=pl.CostEstimate(flops=4 * states.size, bytes_accessed=8 * states.size, transcendentals=0),
        name="anomalies",
    )(states)


def update_side(region, side, lag, centre, beside, pair_ref, mean_ref, out_ref, done_ref, sem):
    levels, members = out_ref.shape[2:]
    half = HC // 2
    rows = half * levels
    cols = pl.ds(region * HC + side * half, half)
    change = (beside.astype(F32) - centre.astype(F32)).astype(BF16)
    pair = pair_ref[lag, cols].reshape(rows, 2 * members)
    moved = jnp.dot(pair, jnp.concatenate([centre, change], axis=0), preferred_element_type=F32)
    mean = mean_ref[lag, cols].reshape(rows, HALF)
    result = jnp.concatenate([mean, mean], axis=1) + moved
    done_ref[...] = result.astype(BF16).reshape(half, levels, members)
    copy = pltpu.make_async_copy(done_ref, out_ref.at[lag, cols], sem)
    copy.start()
    return copy


def update_sides(parts, pair_ref, mean_ref, out_ref, done_ref, sems):
    copies = []
    for i, (region, side, centre, beside) in enumerate(parts):
        for lag in range(out_ref.shape[0]):
            copies.append(update_side(region, side, lag, centre, beside, pair_ref, mean_ref, out_ref,
                                      done_ref.at[i, lag], sems.at[i, lag]))
    for copy in copies:
        copy.wait()


def first_update_kernel(core_ref, mine_ref, pair_ref, mean_ref, out_ref, done_ref, sems):
    core = core_ref[0]
    region = core * (pair_ref.shape[1] // HC - 1)
    near = mine_ref[1]
    parts = [(region, side, near, mine_ref[2 * side]) for side in range(2)]
    parts.append((region + 1 - 2 * core, core, mine_ref[2 - 2 * core], near))
    update_sides(parts, pair_ref, mean_ref, out_ref, done_ref, sems)


def last_update_kernel(core_ref, mine_ref, other_ref, pair_ref, mean_ref, _, out_ref, all_ref, done_ref, sems):
    core = core_ref[0]
    all_ref[pl.ds(3 * core, 3)] = mine_ref[...]
    all_ref[pl.ds(3 * (1 - core), 3)] = other_ref[...]
    regions = pair_ref.shape[1] // HC
    parts = []
    for step in range(1, regions):
        region = step + core * (regions - 1 - 2 * step)
        for side in range(2):
            if step == 1 and side == 0:
                continue
            towards = side + core * (1 - 2 * side)
            parts.append((region, towards, all_ref[region + 1], all_ref[region + 2 * towards]))
    update_sides(parts, pair_ref, mean_ref, out_ref, done_ref, sems)


def update_call(kernel, args, begun, states, count, scratch, name):
    lags, columns, levels, members = states.shape
    half = HC // 2
    vmem = pl.BlockSpec(memory_space=pltpu.VMEM)
    given = [] if begun is None else [begun]
    flops = 2 * count * lags * half * levels * 2 * members * members
    return pl.pallas_call(
        kernel,
        in_specs=[pl.BlockSpec(memory_space=pltpu.SMEM)] + [vmem] * (len(args) - 1) + [pl.BlockSpec(memory_space=pl.ANY)] * len(given),
        out_specs=pl.BlockSpec(memory_space=pl.ANY),
        out_shape=jax.ShapeDtypeStruct(states.shape, BF16),
        scratch_shapes=scratch + [pltpu.VMEM((count, lags, half, levels, members), BF16),
                                  pltpu.SemaphoreType.DMA((count, lags))],
        input_output_aliases={len(args): 0} if given else {},
        compiler_params=pltpu.CompilerParams(vmem_limit_bytes=VMEM_LIMIT),
        cost_estimate=pl.CostEstimate(flops=flops, bytes_accessed=count * lags * half * levels * members * 6, transcendentals=0),
        name=name,
    )(*args, *given)


def first_update(core, mine, pair, mean, states):
    return update_call(first_update_kernel, (core, mine, pair, mean), None, states, 3, [], "first_update")


def last_update(core, mine, other, pair, mean, begun):
    count = 2 * (begun.shape[1] // HC) - 3
    return update_call(last_update_kernel, (core, mine, other, pair, mean), begun, begun, count,
                       [pltpu.VMEM((6, K, K), BF16)], "last_update")


def shards(obs_perturb, innovation, error_weight, obs_column, obs_count, radius, states):
    core = (lax.axis_index("tm") % 2).astype(jnp.int32).reshape(1)
    spaces = lax.axis_size("space")
    terms = observation_terms(innovation, error_weight, obs_column, obs_count, radius)
    send = local_grams(core, terms, obs_perturb[0], BF16, "grams_to_send")
    keep = local_grams(1 - core, terms, obs_perturb[0], F32, "grams_to_keep")
    swap_core = [(0, 1), (1, 0), (2, 3), (3, 2)]
    swap_chip = [(0, 2), (2, 0), (1, 3), (3, 1)]
    recv = lax.ppermute(send, "tm", swap_core)
    edge, mine = split_sums(core, keep, recv)
    perm = []
    for chip in range(2):
        for s in range(spaces):
            low, high = 2 * chip * spaces, (2 * chip + 1) * spaces
            perm.append((high + s, low + (s + 1) % spaces))
            perm.append((low + s, high + (s - 1) % spaces))
    states, edge = lax.optimization_barrier((states, edge))
    halo = lax.ppermute(edge, ("tm", "space"), perm)
    halo, pair, mean = lax.optimization_barrier((halo, *anomalies(states)))
    chip_sum = (mine + halo.astype(F32)).astype(BF16)
    other_chip = lax.ppermute(chip_sum, "tm", swap_chip)
    own = transforms(mine, halo, other_chip)
    beside = lax.ppermute(own, "tm", swap_core)
    begun = first_update(core, own, pair, mean, states)
    return last_update(core, own, beside, pair, mean, begun)


def solution(mesh):
    return jax.shard_map(
        shards,
        mesh=mesh,
        in_specs=(
            P("tm", "space", None, None),
            P("tm", "space", None),
            P("tm", "space", None),
            P("tm", "space", None),
            P("tm", "space"),
            P("space"),
            P("tm", "space", None, None),
        ),
        out_specs=P("tm", "space", None, None),
        check_vma=False,
    )
```

```python
import functools

import jax
import jax.numpy as jnp
from jax import lax
from jax.experimental import pallas as pl
from jax.experimental.pallas import tpu as pltpu
from jax.sharding import PartitionSpec as P

HC = 32
NS_ITERS = 5
INFLATION = 1.1
K = 256
HALF = K // 2
ROWS = HALF + HALF + 16
BF16 = jnp.bfloat16
F32 = jnp.float32
VMEM_LIMIT = 32 * 1024 * 1024


def row_col():
    row = lax.broadcasted_iota(jnp.int32, (HALF, HALF), 0)
    col = lax.broadcasted_iota(jnp.int32, (HALF, HALF), 1)
    return row, col


def tail_row():
    return lax.broadcasted_iota(jnp.int32, (16, HALF), 0)


def observation_terms(innovation, error_weight, obs_column, obs_count, radius):
    column = obs_column[0]
    position = lax.broadcasted_iota(jnp.int32, column.shape, 1)
    base = jnp.where(position < obs_count[0][:, None], error_weight[0], 0.0)
    reach = jnp.maximum(radius[:, None], column).astype(F32)
    return base, base * innovation[0], (column.astype(F32) + (0.5 - 0.5 * HC)) / reach, HC / reach


def gram_kernel(targets, side_ref, base_ref, innov_ref, place_ref, width_ref, obs_ref, out_ref, flip_ref, weight_ref, scaled_ref):
    side = side_ref[0]
    regions = obs_ref.shape[0]
    for m in range(5):
        ratio = jnp.minimum(jnp.abs(place_ref[...] - (m - 2.0) * width_ref[...]), 1.0)
        taper = jnp.square(1.0 - ratio * ratio)
        weight_ref[m] = base_ref[...] * taper
        scaled_ref[m] = innov_ref[...] * taper
    row, col = row_col()
    tail = tail_row()
    vecs = []
    for r in range(regions):
        source = r + side * (regions - 1 - 2 * r)
        obs = obs_ref[source]
        flip_ref[r] = obs.T
        here = pl.ds(source, 1)
        scaled = jnp.concatenate([scaled_ref[m, here, :] for m in (0, 1, 2, 3, 4, 4, 4, 4)], axis=0)
        high = scaled.astype(BF16)
        low = (scaled - high.astype(F32)).astype(BF16)
        vec = jnp.dot(jnp.concatenate([high, low], axis=0), obs, preferred_element_type=F32)
        vecs.append(vec[:8] + vec[8:])
    for t in reversed(targets):
        total = None
        vec = None
        for r in reversed(range(regions)):
            m = t - r
            if not 0 <= m <= 4:
                continue
            source = r + side * (regions - 1 - 2 * r)
            offset = m + side * (4 - 2 * m)
            weighted = (flip_ref[r].astype(F32) * weight_ref[offset, pl.ds(source, 1), :]).astype(BF16)
            part = jnp.dot(weighted, obs_ref[source], preferred_element_type=F32)
            total = part if total is None else total + part
            part = jnp.where(side == 0, vecs[r][m : m + 1], vecs[r][4 - m : 5 - m])
            vec = part if vec is None else vec + part
        i = t - targets[0]
        at = i + side * (len(targets) - 1 - 2 * i)
        out_ref[at, :HALF, :] = total[:HALF, HALF:].astype(out_ref.dtype)
        low = total[HALF:, HALF:]
        out_ref[at, HALF:K, :] = jnp.where(row <= col, total[:HALF, :HALF], low).astype(out_ref.dtype)
        diag = jnp.sum(jnp.where(row == col, low, 0.0), axis=0, keepdims=True)
        rest = jnp.where(tail == 0, diag, jnp.where(tail == 1, vec[:, :HALF], jnp.where(tail == 2, vec[:, HALF:], 0.0)))
        out_ref[at, K:, :] = rest.astype(out_ref.dtype)


def local_grams(side, targets, terms, obs, dtype, name):
    regions, capacity, members = obs.shape
    vmem = pl.BlockSpec(memory_space=pltpu.VMEM)
    return pl.pallas_call(
        functools.partial(gram_kernel, targets),
        in_specs=[pl.BlockSpec(memory_space=pltpu.SMEM)] + [vmem] * 5,
        out_specs=vmem,
        out_shape=jax.ShapeDtypeStruct((len(targets), ROWS, HALF), dtype),
        scratch_shapes=[pltpu.VMEM((regions, members, capacity), BF16)] + [pltpu.VMEM((5, regions, capacity), F32)] * 2,
        compiler_params=pltpu.CompilerParams(vmem_limit_bytes=VMEM_LIMIT),
        cost_estimate=pl.CostEstimate(flops=5 * regions * capacity * K * K,
                                      bytes_accessed=regions * capacity * K, transcendentals=0),
        name=name,
    )(side, *terms, obs)


def join_kernel(core_ref, edge_keep_ref, edge_recv_ref, inner_keep_ref, inner_recv_ref, halo_ref, sum_ref, send_ref):
    core = core_ref[0]
    parts = [(j + core, j + 1 - core, edge_keep_ref, edge_recv_ref) for j in range(2)]
    parts.append((2 - 2 * core, 0, inner_keep_ref, inner_recv_ref))
    for k, at, keep_ref, recv_ref in parts:
        total = keep_ref[at] + recv_ref[at].astype(F32) + halo_ref[k].astype(F32)
        sum_ref[k] = total
        send_ref[k] = total.astype(BF16)


def join_sums(core, *sums):
    vmem = pl.BlockSpec(memory_space=pltpu.VMEM)
    return pl.pallas_call(
        join_kernel,
        in_specs=[pl.BlockSpec(memory_space=pltpu.SMEM)] + [vmem] * len(sums),
        out_specs=[vmem, vmem],
        out_shape=[jax.ShapeDtypeStruct((3, ROWS, HALF), F32),
                   jax.ShapeDtypeStruct((3, ROWS, HALF), BF16)],
        compiler_params=pltpu.CompilerParams(vmem_limit_bytes=2 * 1024 * 1024),
        name="join_sums",
    )(core, *sums)


def identity_mask(n):
    return lax.broadcasted_iota(jnp.int32, (n, n), 0) == lax.broadcasted_iota(jnp.int32, (n, n), 1)


def product(a, b):
    return jnp.dot(a.astype(BF16), b.astype(BF16), preferred_element_type=F32)


def transform_kernel(mine_ref, other_ref, out_ref):
    row, col = row_col()
    on_diagonal = identity_mask(K)
    each = range(mine_ref.shape[0])
    total = lambda a: jnp.sum(jnp.sum(a, axis=0, keepdims=True), axis=1, keepdims=True)
    us, ys, frobs, shrinks, squares, vecs = [], [], [], [], [], []
    for k in each:
        packed = mine_ref[k] + other_ref[k].astype(F32)
        corner = packed[:HALF]
        both = packed[HALF:K] + jnp.where(row == col, (K - 1) / INFLATION, 0.0)
        rest = packed[K : K + 1] + (K - 1) / INFLATION
        first = jnp.where(row == col, both, 0.0)
        mean = (total(first) + jnp.sum(rest, axis=1, keepdims=True)) * (1.0 / K)
        frob = jnp.sqrt(total(2.0 * (corner * corner + both * both) - first * first)
                        + jnp.sum(rest * rest, axis=1, keepdims=True))
        flipped = both.T
        upper = jnp.where(row <= col, both, flipped)
        lower = jnp.where(row > col, both, jnp.where(row == col, rest, flipped))
        system = jnp.concatenate(
            [jnp.concatenate([upper, corner], axis=1),
             jnp.concatenate([corner.T, lower], axis=1)], axis=0)
        u = -0.5 * (system - jnp.where(on_diagonal, mean, 0.0))
        shrink = 1.0 / frob
        us.append(u * shrink)
        ys.append(mean * shrink)
        frobs.append(frob)
        shrinks.append(shrink)
        vecs.append(jnp.concatenate([packed[K + 1 : K + 2], packed[K + 2 : K + 3]], axis=1))
    invs = [None for k in each]
    iotas = [1.0 for k in each]
    for iteration in range(NS_ITERS):
        last = iteration == NS_ITERS - 1
        halves = [us[k].astype(BF16) for k in each]
        if not last:
            squares = [product(halves[k], halves[k]) for k in each]
        crosses = [None if invs[k] is None else product(invs[k], halves[k]) for k in each]
        for k in each:
            u, y = us[k], ys[k]
            mu = 1.5 - 0.5 * y
            invs[k] = u if invs[k] is None else mu * invs[k] + iotas[k] * u + crosses[k]
            if not last:
                us[k] = (mu * (1.5 - 1.5 * y)) * u + (3.0 - 1.5 * y) * squares[k] + product(halves[k], squares[k])
            ys[k], iotas[k] = y * mu * mu, iotas[k] * mu
    for k in each:
        inverse = invs[k] + jnp.where(on_diagonal, iotas[k], 0.0)
        vec_col = jnp.broadcast_to(vecs[k], (HALF, K)).T[:, :1]
        half_step = jnp.sum(inverse * vec_col, axis=0, keepdims=True)
        wbar = jnp.sum(inverse * half_step, axis=1, keepdims=True) * shrinks[k]
        scale = (K - 1.0) ** 0.5 / jnp.sqrt(frobs[k])
        out_ref[k] = (scale * inverse + wbar).astype(BF16)


def transforms(mine, other):
    vmem = pl.BlockSpec(memory_space=pltpu.VMEM)
    return pl.pallas_call(
        transform_kernel,
        in_specs=[vmem, vmem],
        out_specs=vmem,
        out_shape=jax.ShapeDtypeStruct((mine.shape[0], K, K), BF16),
        compiler_params=pltpu.CompilerParams(vmem_limit_bytes=VMEM_LIMIT),
        name="transforms",
    )(mine, other)


def anomaly_kernel(states_ref, pair_ref, mean_ref):
    lags, columns, levels, members = states_ref.shape
    rows = lags * columns * levels
    state = states_ref[...].reshape(rows, members).astype(F32)
    mean = jnp.mean(state, axis=1, keepdims=True)
    anomaly = (state - mean).astype(BF16).reshape(states_ref.shape)
    column = lax.broadcasted_iota(jnp.int32, states_ref.shape, 1)
    blend = jnp.abs((column.astype(F32) + 0.5) / columns - 0.5)
    pair_ref[:, :, :, :members] = anomaly
    pair_ref[:, :, :, members:] = (anomaly.astype(F32) * blend).astype(BF16)
    mean_ref[...] = jnp.broadcast_to(mean, (rows, HALF)).reshape(mean_ref.shape)


def anomalies(states):
    lags, columns, levels, members = states.shape
    block = lambda width: pl.BlockSpec((lags, HC, levels, width), lambda r: (0, r, 0, 0))
    return pl.pallas_call(
        anomaly_kernel,
        grid=(columns // HC,),
        in_specs=[block(members)],
        out_specs=[block(2 * members), block(HALF)],
        out_shape=[jax.ShapeDtypeStruct(states.shape[:-1] + (2 * members,), BF16),
                   jax.ShapeDtypeStruct(states.shape[:-1] + (HALF,), F32)],
        compiler_params=pltpu.CompilerParams(vmem_limit_bytes=VMEM_LIMIT),
        cost_estimate=pl.CostEstimate(flops=4 * states.size, bytes_accessed=8 * states.size, transcendentals=0),
        name="anomalies",
    )(states)


def update_side(region, side, lag, centre, beside, pair_ref, mean_ref, out_ref, done_ref, sem):
    levels, members = out_ref.shape[2:]
    half = HC // 2
    rows = half * levels
    cols = pl.ds(region * HC + side * half, half)
    change = (beside.astype(F32) - centre.astype(F32)).astype(BF16)
    pair = pair_ref[lag, cols].reshape(rows, 2 * members)
    moved = jnp.dot(pair, jnp.concatenate([centre, change], axis=0), preferred_element_type=F32)
    mean = mean_ref[lag, cols].reshape(rows, HALF)
    result = jnp.concatenate([mean, mean], axis=1) + moved
    done_ref[...] = result.astype(BF16).reshape(half, levels, members)
    copy = pltpu.make_async_copy(done_ref, out_ref.at[lag, cols], sem)
    copy.start()
    return copy


def update_sides(parts, pair_ref, mean_ref, out_ref, done_ref, sems):
    copies = []
    for i, (region, side, centre, beside) in enumerate(parts):
        for lag in range(out_ref.shape[0]):
            copies.append(update_side(region, side, lag, centre, beside, pair_ref, mean_ref, out_ref,
                                      done_ref.at[i, lag], sems.at[i, lag]))
    for copy in copies:
        copy.wait()


def first_update_kernel(core_ref, mine_ref, pair_ref, mean_ref, out_ref, done_ref, sems):
    core = core_ref[0]
    region = core * (pair_ref.shape[1] // HC - 1)
    near = mine_ref[1]
    parts = [(region, side, near, mine_ref[2 * side]) for side in range(2)]
    parts.append((region + 1 - 2 * core, core, mine_ref[2 - 2 * core], near))
    update_sides(parts, pair_ref, mean_ref, out_ref, done_ref, sems)


def last_update_kernel(core_ref, mine_ref, other_ref, pair_ref, mean_ref, _, out_ref, all_ref, done_ref, sems):
    core = core_ref[0]
    all_ref[pl.ds(3 * core, 3)] = mine_ref[...]
    all_ref[pl.ds(3 * (1 - core), 3)] = other_ref[...]
    regions = pair_ref.shape[1] // HC
    parts = []
    for step in range(1, regions):
        region = step + core * (regions - 1 - 2 * step)
        for side in range(2):
            if step == 1 and side == 0:
                continue
            towards = side + core * (1 - 2 * side)
            parts.append((region, towards, all_ref[region + 1], all_ref[region + 2 * towards]))
    update_sides(parts, pair_ref, mean_ref, out_ref, done_ref, sems)


def update_call(kernel, args, begun, states, count, scratch, name):
    lags, columns, levels, members = states.shape
    half = HC // 2
    vmem = pl.BlockSpec(memory_space=pltpu.VMEM)
    given = [] if begun is None else [begun]
    flops = 2 * count * lags * half * levels * 2 * members * members
    return pl.pallas_call(
        kernel,
        in_specs=[pl.BlockSpec(memory_space=pltpu.SMEM)] + [vmem] * (len(args) - 1) + [pl.BlockSpec(memory_space=pl.ANY)] * len(given),
        out_specs=pl.BlockSpec(memory_space=pl.ANY),
        out_shape=jax.ShapeDtypeStruct(states.shape, BF16),
        scratch_shapes=scratch + [pltpu.VMEM((count, lags, half, levels, members), BF16),
                                  pltpu.SemaphoreType.DMA((count, lags))],
        input_output_aliases={len(args): 0} if given else {},
        compiler_params=pltpu.CompilerParams(vmem_limit_bytes=VMEM_LIMIT),
        cost_estimate=pl.CostEstimate(flops=flops, bytes_accessed=count * lags * half * levels * members * 6, transcendentals=0),
        name=name,
    )(*args, *given)


def first_update(core, mine, pair, mean, states):
    return update_call(first_update_kernel, (core, mine, pair, mean), None, states, 3, [], "first_update")


def last_update(core, mine, other, pair, mean, begun):
    count = 2 * (begun.shape[1] // HC) - 3
    return update_call(last_update_kernel, (core, mine, other, pair, mean), begun, begun, count,
                       [pltpu.VMEM((6, K, K), BF16)], "last_update")


def shards(obs_perturb, innovation, error_weight, obs_column, obs_count, radius, states):
    core = (lax.axis_index("tm") % 2).astype(jnp.int32).reshape(1)
    spaces = lax.axis_size("space")
    terms = observation_terms(innovation, error_weight, obs_column, obs_count, radius)
    swap_core = [(0, 1), (1, 0), (2, 3), (3, 2)]
    swap_chip = [(0, 2), (2, 0), (1, 3), (3, 1)]
    up_down = []
    for chip in range(2):
        for s in range(spaces):
            low, high = 2 * chip * spaces, (2 * chip + 1) * spaces
            up_down.append((high + s, low + (s + 1) % spaces))
            up_down.append((low + s, high + (s - 1) % spaces))
    send = local_grams(core, (5, 6, 7), terms, obs_perturb[0], BF16, "edges_to_send")
    recv = lax.ppermute(send, "tm", swap_core)
    keep = local_grams(1 - core, (5, 6, 7), terms, obs_perturb[0], F32, "edges_to_keep")
    edge = (keep + recv.astype(F32)).astype(BF16)
    halo = lax.ppermute(edge, ("tm", "space"), up_down)
    _, later = lax.optimization_barrier((edge, core))
    inner_send = local_grams(later, (4,), terms, obs_perturb[0], BF16, "inner_to_send")
    inner_recv = lax.ppermute(inner_send, "tm", swap_core)
    inner_keep = local_grams(1 - later, (4,), terms, obs_perturb[0], F32, "inner_to_keep")
    total, chip_sum = join_sums(core, keep, recv, inner_keep, inner_recv, halo)
    states, chip_sum = lax.optimization_barrier((states, chip_sum))
    other_chip = lax.ppermute(chip_sum, "tm", swap_chip)
    other_chip, pair, mean = lax.optimization_barrier((other_chip, *anomalies(states)))
    own = transforms(total, other_chip)
    beside = lax.ppermute(own, "tm", swap_core)
    begun = first_update(core, own, pair, mean, states)
    return last_update(core, own, beside, pair, mean, begun)


def solution(mesh):
    return jax.shard_map(
        shards,
        mesh=mesh,
        in_specs=(
            P("tm", "space", None, None),
            P("tm", "space", None),
            P("tm", "space", None),
            P("tm", "space", None),
            P("tm", "space"),
            P("space"),
            P("tm", "space", None, None),
        ),
        out_specs=P("tm", "space", None, None),
        check_vma=False,
    )
```

```python
import functools

import jax
import jax.numpy as jnp
from jax import lax
from jax.experimental import pallas as pl
from jax.experimental.pallas import tpu as pltpu
from jax.sharding import PartitionSpec as P

HC = 32
NS_ITERS = 5
INFLATION = 1.1
K = 256
HALF = K // 2
ROWS = HALF + HALF + 16
BF16 = jnp.bfloat16
F32 = jnp.float32
VMEM_LIMIT = 32 * 1024 * 1024


def row_col():
    row = lax.broadcasted_iota(jnp.int32, (HALF, HALF), 0)
    col = lax.broadcasted_iota(jnp.int32, (HALF, HALF), 1)
    return row, col


def tail_row():
    return lax.broadcasted_iota(jnp.int32, (16, HALF), 0)


def observation_terms(innovation, error_weight, obs_column, obs_count, radius):
    column = obs_column[0]
    position = lax.broadcasted_iota(jnp.int32, column.shape, 1)
    base = jnp.where(position < obs_count[0][:, None], error_weight[0], 0.0)
    reach = jnp.maximum(radius[:, None], column).astype(F32)
    return base, base * innovation[0], (column.astype(F32) + (0.5 - 0.5 * HC)) / reach, HC / reach


def gram_kernel(targets, side_ref, base_ref, innov_ref, place_ref, width_ref, obs_ref, out_ref, flip_ref, weight_ref, scaled_ref):
    side = side_ref[0]
    regions = obs_ref.shape[0]
    for m in range(5):
        ratio = jnp.minimum(jnp.abs(place_ref[...] - (m - 2.0) * width_ref[...]), 1.0)
        taper = jnp.square(1.0 - ratio * ratio)
        weight_ref[m] = base_ref[...] * taper
        scaled_ref[m] = innov_ref[...] * taper
    row, col = row_col()
    tail = tail_row()
    vecs = {}
    for r in reversed(range(regions)):
        if not any(0 <= t - r <= 4 for t in targets):
            continue
        source = r + side * (regions - 1 - 2 * r)
        obs = obs_ref[source]
        flip_ref[r] = obs.T
        here = pl.ds(source, 1)
        scaled = jnp.concatenate([scaled_ref[m, here, :] for m in (0, 1, 2, 3, 4, 4, 4, 4)], axis=0)
        high = scaled.astype(BF16)
        low = (scaled - high.astype(F32)).astype(BF16)
        vec = jnp.dot(jnp.concatenate([high, low], axis=0), obs, preferred_element_type=F32)
        vecs[r] = vec[:8] + vec[8:]
    for t in reversed(targets):
        total = None
        vec = None
        for r in reversed(range(regions)):
            m = t - r
            if not 0 <= m <= 4:
                continue
            source = r + side * (regions - 1 - 2 * r)
            offset = m + side * (4 - 2 * m)
            weighted = (flip_ref[r].astype(F32) * weight_ref[offset, pl.ds(source, 1), :]).astype(BF16)
            part = jnp.dot(weighted, obs_ref[source], preferred_element_type=F32)
            total = part if total is None else total + part
            part = jnp.where(side == 0, vecs[r][m : m + 1], vecs[r][4 - m : 5 - m])
            vec = part if vec is None else vec + part
        i = t - targets[0]
        at = i + side * (len(targets) - 1 - 2 * i)
        out_ref[at, :HALF, :] = total[:HALF, HALF:].astype(out_ref.dtype)
        low = total[HALF:, HALF:]
        out_ref[at, HALF:K, :] = jnp.where(row <= col, total[:HALF, :HALF], low).astype(out_ref.dtype)
        diag = jnp.sum(jnp.where(row == col, low, 0.0), axis=0, keepdims=True)
        rest = jnp.where(tail == 0, diag, jnp.where(tail == 1, vec[:, :HALF], jnp.where(tail == 2, vec[:, HALF:], 0.0)))
        out_ref[at, K:, :] = rest.astype(out_ref.dtype)


def local_grams(side, targets, terms, obs, dtype, name):
    regions, capacity, members = obs.shape
    vmem = pl.BlockSpec(memory_space=pltpu.VMEM)
    return pl.pallas_call(
        functools.partial(gram_kernel, targets),
        in_specs=[pl.BlockSpec(memory_space=pltpu.SMEM)] + [vmem] * 5,
        out_specs=vmem,
        out_shape=jax.ShapeDtypeStruct((len(targets), ROWS, HALF), dtype),
        scratch_shapes=[pltpu.VMEM((regions, members, capacity), BF16)] + [pltpu.VMEM((5, regions, capacity), F32)] * 2,
        compiler_params=pltpu.CompilerParams(vmem_limit_bytes=VMEM_LIMIT),
        cost_estimate=pl.CostEstimate(flops=5 * regions * capacity * K * K,
                                      bytes_accessed=regions * capacity * K, transcendentals=0),
        name=name,
    )(side, *terms, obs)


def join_kernel(core_ref, edge_keep_ref, edge_recv_ref, inner_keep_ref, inner_recv_ref, halo_ref, sum_ref, send_ref):
    core = core_ref[0]
    parts = [(j + core, j + 1 - core, edge_keep_ref, edge_recv_ref) for j in range(2)]
    parts.append((2 - 2 * core, 0, inner_keep_ref, inner_recv_ref))
    for k, at, keep_ref, recv_ref in parts:
        total = keep_ref[at] + recv_ref[at].astype(F32) + halo_ref[k].astype(F32)
        sum_ref[k] = total
        send_ref[k] = total.astype(BF16)


def join_sums(core, *sums):
    vmem = pl.BlockSpec(memory_space=pltpu.VMEM)
    return pl.pallas_call(
        join_kernel,
        in_specs=[pl.BlockSpec(memory_space=pltpu.SMEM)] + [vmem] * len(sums),
        out_specs=[vmem, vmem],
        out_shape=[jax.ShapeDtypeStruct((3, ROWS, HALF), F32),
                   jax.ShapeDtypeStruct((3, ROWS, HALF), BF16)],
        compiler_params=pltpu.CompilerParams(vmem_limit_bytes=2 * 1024 * 1024),
        name="join_sums",
    )(core, *sums)


def identity_mask(n):
    return lax.broadcasted_iota(jnp.int32, (n, n), 0) == lax.broadcasted_iota(jnp.int32, (n, n), 1)


def product(a, b):
    return jnp.dot(a.astype(BF16), b.astype(BF16), preferred_element_type=F32)


def transform_kernel(mine_ref, other_ref, out_ref):
    row, col = row_col()
    on_diagonal = identity_mask(K)
    each = range(mine_ref.shape[0])
    total = lambda a: jnp.sum(jnp.sum(a, axis=0, keepdims=True), axis=1, keepdims=True)
    us, ys, frobs, shrinks, squares, vecs = [], [], [], [], [], []
    for k in each:
        packed = mine_ref[k] + other_ref[k].astype(F32)
        corner = packed[:HALF]
        both = packed[HALF:K] + jnp.where(row == col, (K - 1) / INFLATION, 0.0)
        rest = packed[K : K + 1] + (K - 1) / INFLATION
        first = jnp.where(row == col, both, 0.0)
        mean = (total(first) + jnp.sum(rest, axis=1, keepdims=True)) * (1.0 / K)
        frob = jnp.sqrt(total(2.0 * (corner * corner + both * both) - first * first)
                        + jnp.sum(rest * rest, axis=1, keepdims=True))
        flipped = both.T
        upper = jnp.where(row <= col, both, flipped)
        lower = jnp.where(row > col, both, jnp.where(row == col, rest, flipped))
        system = jnp.concatenate(
            [jnp.concatenate([upper, corner], axis=1),
             jnp.concatenate([corner.T, lower], axis=1)], axis=0)
        u = -0.5 * (system - jnp.where(on_diagonal, mean, 0.0))
        shrink = 1.0 / frob
        us.append(u * shrink)
        ys.append(mean * shrink)
        frobs.append(frob)
        shrinks.append(shrink)
        vecs.append(jnp.concatenate([packed[K + 1 : K + 2], packed[K + 2 : K + 3]], axis=1))
    invs = [None for k in each]
    iotas = [1.0 for k in each]
    for iteration in range(NS_ITERS):
        last = iteration == NS_ITERS - 1
        halves = [us[k].astype(BF16) for k in each]
        if not last:
            squares = [product(halves[k], halves[k]) for k in each]
        crosses = [None if invs[k] is None else product(invs[k], halves[k]) for k in each]
        for k in each:
            u, y = us[k], ys[k]
            mu = 1.5 - 0.5 * y
            invs[k] = u if invs[k] is None else mu * invs[k] + iotas[k] * u + crosses[k]
            if not last:
                us[k] = (mu * (1.5 - 1.5 * y)) * u + (3.0 - 1.5 * y) * squares[k] + product(halves[k], squares[k])
            ys[k], iotas[k] = y * mu * mu, iotas[k] * mu
    for k in each:
        inverse = invs[k] + jnp.where(on_diagonal, iotas[k], 0.0)
        vec_col = jnp.broadcast_to(vecs[k], (HALF, K)).T[:, :1]
        half_step = jnp.sum(inverse * vec_col, axis=0, keepdims=True)
        wbar = jnp.sum(inverse * half_step, axis=1, keepdims=True) * shrinks[k]
        scale = (K - 1.0) ** 0.5 / jnp.sqrt(frobs[k])
        out_ref[k] = (scale * inverse + wbar).astype(BF16)


def transforms(mine, other):
    vmem = pl.BlockSpec(memory_space=pltpu.VMEM)
    return pl.pallas_call(
        transform_kernel,
        in_specs=[vmem, vmem],
        out_specs=vmem,
        out_shape=jax.ShapeDtypeStruct((mine.shape[0], K, K), BF16),
        compiler_params=pltpu.CompilerParams(vmem_limit_bytes=VMEM_LIMIT),
        name="transforms",
    )(mine, other)


def anomaly_kernel(states_ref, pair_ref, mean_ref):
    lags, columns, levels, members = states_ref.shape
    rows = lags * columns * levels
    state = states_ref[...].reshape(rows, members).astype(F32)
    mean = jnp.mean(state, axis=1, keepdims=True)
    anomaly = (state - mean).astype(BF16).reshape(states_ref.shape)
    column = lax.broadcasted_iota(jnp.int32, states_ref.shape, 1)
    blend = jnp.abs((column.astype(F32) + 0.5) / columns - 0.5)
    pair_ref[:, :, :, :members] = anomaly
    pair_ref[:, :, :, members:] = (anomaly.astype(F32) * blend).astype(BF16)
    mean_ref[...] = jnp.broadcast_to(mean, (rows, HALF)).reshape(mean_ref.shape)


def anomalies(states):
    lags, columns, levels, members = states.shape
    block = lambda width: pl.BlockSpec((lags, HC, levels, width), lambda r: (0, r, 0, 0))
    return pl.pallas_call(
        anomaly_kernel,
        grid=(columns // HC,),
        in_specs=[block(members)],
        out_specs=[block(2 * members), block(HALF)],
        out_shape=[jax.ShapeDtypeStruct(states.shape[:-1] + (2 * members,), BF16),
                   jax.ShapeDtypeStruct(states.shape[:-1] + (HALF,), F32)],
        compiler_params=pltpu.CompilerParams(vmem_limit_bytes=VMEM_LIMIT),
        cost_estimate=pl.CostEstimate(flops=4 * states.size, bytes_accessed=8 * states.size, transcendentals=0),
        name="anomalies",
    )(states)


def update_side(region, side, lag, centre, beside, pair_ref, mean_ref, out_ref, done_ref, sem):
    levels, members = out_ref.shape[2:]
    half = HC // 2
    rows = half * levels
    cols = pl.ds(region * HC + side * half, half)
    change = (beside.astype(F32) - centre.astype(F32)).astype(BF16)
    pair = pair_ref[lag, cols].reshape(rows, 2 * members)
    moved = jnp.dot(pair, jnp.concatenate([centre, change], axis=0), preferred_element_type=F32)
    mean = mean_ref[lag, cols].reshape(rows, HALF)
    result = jnp.concatenate([mean, mean], axis=1) + moved
    done_ref[...] = result.astype(BF16).reshape(half, levels, members)
    copy = pltpu.make_async_copy(done_ref, out_ref.at[lag, cols], sem)
    copy.start()
    return copy


def update_sides(parts, pair_ref, mean_ref, out_ref, done_ref, sems):
    copies = []
    for i, (region, side, centre, beside) in enumerate(parts):
        for lag in range(out_ref.shape[0]):
            copies.append(update_side(region, side, lag, centre, beside, pair_ref, mean_ref, out_ref,
                                      done_ref.at[i, lag], sems.at[i, lag]))
    for copy in copies:
        copy.wait()


def first_update_kernel(core_ref, mine_ref, pair_ref, mean_ref, out_ref, done_ref, sems):
    core = core_ref[0]
    region = core * (pair_ref.shape[1] // HC - 1)
    near = mine_ref[1]
    parts = [(region, side, near, mine_ref[2 * side]) for side in range(2)]
    parts.append((region + 1 - 2 * core, core, mine_ref[2 - 2 * core], near))
    update_sides(parts, pair_ref, mean_ref, out_ref, done_ref, sems)


def last_update_kernel(core_ref, mine_ref, other_ref, pair_ref, mean_ref, _, out_ref, all_ref, done_ref, sems):
    core = core_ref[0]
    all_ref[pl.ds(3 * core, 3)] = mine_ref[...]
    all_ref[pl.ds(3 * (1 - core), 3)] = other_ref[...]
    regions = pair_ref.shape[1] // HC
    parts = []
    for step in range(1, regions):
        region = step + core * (regions - 1 - 2 * step)
        for side in range(2):
            if step == 1 and side == 0:
                continue
            towards = side + core * (1 - 2 * side)
            parts.append((region, towards, all_ref[region + 1], all_ref[region + 2 * towards]))
    update_sides(parts, pair_ref, mean_ref, out_ref, done_ref, sems)


def update_call(kernel, args, begun, states, count, scratch, name):
    lags, columns, levels, members = states.shape
    half = HC // 2
    vmem = pl.BlockSpec(memory_space=pltpu.VMEM)
    given = [] if begun is None else [begun]
    flops = 2 * count * lags * half * levels * 2 * members * members
    return pl.pallas_call(
        kernel,
        in_specs=[pl.BlockSpec(memory_space=pltpu.SMEM)] + [vmem] * (len(args) - 1) + [pl.BlockSpec(memory_space=pl.ANY)] * len(given),
        out_specs=pl.BlockSpec(memory_space=pl.ANY),
        out_shape=jax.ShapeDtypeStruct(states.shape, BF16),
        scratch_shapes=scratch + [pltpu.VMEM((count, lags, half, levels, members), BF16),
                                  pltpu.SemaphoreType.DMA((count, lags))],
        input_output_aliases={len(args): 0} if given else {},
        compiler_params=pltpu.CompilerParams(vmem_limit_bytes=VMEM_LIMIT),
        cost_estimate=pl.CostEstimate(flops=flops, bytes_accessed=count * lags * half * levels * members * 6, transcendentals=0),
        name=name,
    )(*args, *given)


def first_update(core, mine, pair, mean, states):
    return update_call(first_update_kernel, (core, mine, pair, mean), None, states, 3, [], "first_update")


def last_update(core, mine, other, pair, mean, begun):
    count = 2 * (begun.shape[1] // HC) - 3
    return update_call(last_update_kernel, (core, mine, other, pair, mean), begun, begun, count,
                       [pltpu.VMEM((6, K, K), BF16)], "last_update")


def shards(obs_perturb, innovation, error_weight, obs_column, obs_count, radius, states):
    core = (lax.axis_index("tm") % 2).astype(jnp.int32).reshape(1)
    spaces = lax.axis_size("space")
    terms = observation_terms(innovation, error_weight, obs_column, obs_count, radius)
    swap_core = [(0, 1), (1, 0), (2, 3), (3, 2)]
    swap_chip = [(0, 2), (2, 0), (1, 3), (3, 1)]
    up_down = []
    for chip in range(2):
        for s in range(spaces):
            following = (s + 1) % spaces
            there = 1 - chip if following % (spaces // 2) == 0 else chip
            upper, lower = (2 * chip + 1) * spaces + s, 2 * there * spaces + following
            up_down += [(upper, lower), (lower, upper)]
    send = local_grams(core, (5, 6, 7), terms, obs_perturb[0], BF16, "edges_to_send")
    recv = lax.ppermute(send, "tm", swap_core)
    keep = local_grams(1 - core, (5, 6, 7), terms, obs_perturb[0], F32, "edges_to_keep")
    edge = (keep + recv.astype(F32)).astype(BF16)
    halo = lax.ppermute(edge, ("tm", "space"), up_down)
    _, later = lax.optimization_barrier((edge, core))
    inner_send = local_grams(later, (4,), terms, obs_perturb[0], BF16, "inner_to_send")
    inner_recv = lax.ppermute(inner_send, "tm", swap_core)
    inner_keep = local_grams(1 - later, (4,), terms, obs_perturb[0], F32, "inner_to_keep")
    total, chip_sum = join_sums(core, keep, recv, inner_keep, inner_recv, halo)
    states, chip_sum = lax.optimization_barrier((states, chip_sum))
    other_chip = lax.ppermute(chip_sum, "tm", swap_chip)
    other_chip, pair, mean = lax.optimization_barrier((other_chip, *anomalies(states)))
    own = transforms(total, other_chip)
    beside = lax.ppermute(own, "tm", swap_core)
    begun = first_update(core, own, pair, mean, states)
    return last_update(core, own, beside, pair, mean, begun)


def solution(mesh):
    return jax.shard_map(
        shards,
        mesh=mesh,
        in_specs=(
            P("tm", "space", None, None),
            P("tm", "space", None),
            P("tm", "space", None),
            P("tm", "space", None),
            P("tm", "space"),
            P("space"),
            P("tm", "space", None, None),
        ),
        out_specs=P("tm", "space", None, None),
        check_vma=False,
    )
```

```python
import functools

import jax
import jax.numpy as jnp
from jax import lax
from jax.experimental import pallas as pl
from jax.experimental.pallas import tpu as pltpu
from jax.sharding import PartitionSpec as P

HC = 32
NS_ITERS = 5
INFLATION = 1.1
K = 256
HALF = K // 2
ROWS = HALF + HALF + 16
BF16 = jnp.bfloat16
F32 = jnp.float32
VMEM_LIMIT = 32 * 1024 * 1024


def row_col():
    row = lax.broadcasted_iota(jnp.int32, (HALF, HALF), 0)
    col = lax.broadcasted_iota(jnp.int32, (HALF, HALF), 1)
    return row, col


def tail_row():
    return lax.broadcasted_iota(jnp.int32, (16, HALF), 0)


def observation_terms(innovation, error_weight, obs_column, obs_count, radius):
    column = obs_column[0]
    position = lax.broadcasted_iota(jnp.int32, column.shape, 1)
    base = jnp.where(position < obs_count[0][:, None], error_weight[0], 0.0)
    reach = jnp.maximum(radius[:, None], column).astype(F32)
    return base, base * innovation[0], (column.astype(F32) + (0.5 - 0.5 * HC)) / reach, HC / reach


def gram_kernel(targets, side_ref, base_ref, innov_ref, place_ref, width_ref, obs_ref, out_ref, flip_ref, weight_ref, scaled_ref):
    side = side_ref[0]
    regions = obs_ref.shape[0]
    for m in range(5):
        ratio = jnp.minimum(jnp.abs(place_ref[...] - (m - 2.0) * width_ref[...]), 1.0)
        taper = jnp.square(1.0 - ratio * ratio)
        weight_ref[m] = base_ref[...] * taper
        scaled_ref[m] = innov_ref[...] * taper
    row, col = row_col()
    tail = tail_row()
    vecs = {}
    for r in range(regions):
        if any(0 <= t - r <= 4 for t in targets):
            flip_ref[r] = obs_ref[r + side * (regions - 1 - 2 * r)].T
    for t in reversed(targets):
        total = None
        vec = None
        for r in reversed(range(regions)):
            m = t - r
            if not 0 <= m <= 4:
                continue
            source = r + side * (regions - 1 - 2 * r)
            offset = m + side * (4 - 2 * m)
            weighted = (flip_ref[r].astype(F32) * weight_ref[offset, pl.ds(source, 1), :]).astype(BF16)
            if r not in vecs:
                here = pl.ds(source, 1)
                scaled = jnp.concatenate([scaled_ref[k, here, :] for k in (0, 1, 2, 3, 4, 4, 4, 4)], axis=0)
                high = scaled.astype(BF16)
                low = (scaled - high.astype(F32)).astype(BF16)
                weighted = jnp.concatenate([weighted, jnp.concatenate([high, low], axis=0)], axis=0)
            part = jnp.dot(weighted, obs_ref[source], preferred_element_type=F32)
            if r not in vecs:
                vecs[r] = part[K : K + 8] + part[K + 8 :]
                part = part[:K]
            total = part if total is None else total + part
            part = jnp.where(side == 0, vecs[r][m : m + 1], vecs[r][4 - m : 5 - m])
            vec = part if vec is None else vec + part
        i = t - targets[0]
        at = i + side * (len(targets) - 1 - 2 * i)
        out_ref[at, :HALF, :] = total[:HALF, HALF:].astype(out_ref.dtype)
        low = total[HALF:, HALF:]
        out_ref[at, HALF:K, :] = jnp.where(row <= col, total[:HALF, :HALF], low).astype(out_ref.dtype)
        diag = jnp.sum(jnp.where(row == col, low, 0.0), axis=0, keepdims=True)
        rest = jnp.where(tail == 0, diag, jnp.where(tail == 1, vec[:, :HALF], jnp.where(tail == 2, vec[:, HALF:], 0.0)))
        out_ref[at, K:, :] = rest.astype(out_ref.dtype)


def local_grams(side, targets, terms, obs, dtype, name):
    regions, capacity, members = obs.shape
    vmem = pl.BlockSpec(memory_space=pltpu.VMEM)
    return pl.pallas_call(
        functools.partial(gram_kernel, targets),
        in_specs=[pl.BlockSpec(memory_space=pltpu.SMEM)] + [vmem] * 5,
        out_specs=vmem,
        out_shape=jax.ShapeDtypeStruct((len(targets), ROWS, HALF), dtype),
        scratch_shapes=[pltpu.VMEM((regions, members, capacity), BF16)] + [pltpu.VMEM((5, regions, capacity), F32)] * 2,
        compiler_params=pltpu.CompilerParams(vmem_limit_bytes=VMEM_LIMIT),
        cost_estimate=pl.CostEstimate(flops=5 * regions * capacity * K * K,
                                      bytes_accessed=regions * capacity * K, transcendentals=0),
        name=name,
    )(side, *terms, obs)


def join_kernel(core_ref, edge_keep_ref, edge_recv_ref, inner_keep_ref, inner_recv_ref, halo_ref, sum_ref, send_ref):
    core = core_ref[0]
    parts = [(j + core, j + 1 - core, edge_keep_ref, edge_recv_ref) for j in range(2)]
    parts.append((2 - 2 * core, 0, inner_keep_ref, inner_recv_ref))
    for k, at, keep_ref, recv_ref in parts:
        total = keep_ref[at] + recv_ref[at].astype(F32) + halo_ref[k].astype(F32)
        sum_ref[k] = total
        send_ref[k] = total.astype(BF16)


def join_sums(core, *sums):
    vmem = pl.BlockSpec(memory_space=pltpu.VMEM)
    return pl.pallas_call(
        join_kernel,
        in_specs=[pl.BlockSpec(memory_space=pltpu.SMEM)] + [vmem] * len(sums),
        out_specs=[vmem, vmem],
        out_shape=[jax.ShapeDtypeStruct((3, ROWS, HALF), F32),
                   jax.ShapeDtypeStruct((3, ROWS, HALF), BF16)],
        compiler_params=pltpu.CompilerParams(vmem_limit_bytes=2 * 1024 * 1024),
        name="join_sums",
    )(core, *sums)


def identity_mask(n):
    return lax.broadcasted_iota(jnp.int32, (n, n), 0) == lax.broadcasted_iota(jnp.int32, (n, n), 1)


def product(a, b):
    return jnp.dot(a.astype(BF16), b.astype(BF16), preferred_element_type=F32)


def transform_kernel(mine_ref, other_ref, out_ref):
    row, col = row_col()
    on_diagonal = identity_mask(K)
    each = range(mine_ref.shape[0])
    total = lambda a: jnp.sum(jnp.sum(a, axis=0, keepdims=True), axis=1, keepdims=True)
    us, ys, frobs, shrinks, squares, vecs = [], [], [], [], [], []
    for k in each:
        packed = mine_ref[k] + other_ref[k].astype(F32)
        corner = packed[:HALF]
        both = packed[HALF:K] + jnp.where(row == col, (K - 1) / INFLATION, 0.0)
        rest = packed[K : K + 1] + (K - 1) / INFLATION
        first = jnp.where(row == col, both, 0.0)
        mean = (total(first) + jnp.sum(rest, axis=1, keepdims=True)) * (1.0 / K)
        frob = jnp.sqrt(total(2.0 * (corner * corner + both * both) - first * first)
                        + jnp.sum(rest * rest, axis=1, keepdims=True))
        flipped = both.T
        upper = jnp.where(row <= col, both, flipped)
        lower = jnp.where(row > col, both, jnp.where(row == col, rest, flipped))
        system = jnp.concatenate(
            [jnp.concatenate([upper, corner], axis=1),
             jnp.concatenate([corner.T, lower], axis=1)], axis=0)
        u = -0.5 * (system - jnp.where(on_diagonal, mean, 0.0))
        shrink = 1.0 / frob
        us.append(u * shrink)
        ys.append(mean * shrink)
        frobs.append(frob)
        shrinks.append(shrink)
        vecs.append(jnp.concatenate([packed[K + 1 : K + 2], packed[K + 2 : K + 3]], axis=1))
    invs = [None for k in each]
    iotas = [1.0 for k in each]
    for iteration in range(NS_ITERS):
        last = iteration == NS_ITERS - 1
        halves = [us[k].astype(BF16) for k in each]
        if not last:
            squares = [product(halves[k], halves[k]) for k in each]
        crosses = [None if invs[k] is None else product(invs[k], halves[k]) for k in each]
        for k in each:
            u, y = us[k], ys[k]
            mu = 1.5 - 0.5 * y
            invs[k] = u if invs[k] is None else mu * invs[k] + iotas[k] * u + crosses[k]
            if not last:
                us[k] = (mu * (1.5 - 1.5 * y)) * u + (3.0 - 1.5 * y) * squares[k] + product(halves[k], squares[k])
            ys[k], iotas[k] = y * mu * mu, iotas[k] * mu
    for k in each:
        inverse = invs[k] + jnp.where(on_diagonal, iotas[k], 0.0)
        vec_col = jnp.broadcast_to(vecs[k], (HALF, K)).T[:, :1]
        half_step = jnp.sum(inverse * vec_col, axis=0, keepdims=True)
        wbar = jnp.sum(inverse * half_step, axis=1, keepdims=True) * shrinks[k]
        scale = (K - 1.0) ** 0.5 / jnp.sqrt(frobs[k])
        out_ref[k] = (scale * inverse + wbar).astype(BF16)


def transforms(mine, other):
    vmem = pl.BlockSpec(memory_space=pltpu.VMEM)
    return pl.pallas_call(
        transform_kernel,
        in_specs=[vmem, vmem],
        out_specs=vmem,
        out_shape=jax.ShapeDtypeStruct((mine.shape[0], K, K), BF16),
        compiler_params=pltpu.CompilerParams(vmem_limit_bytes=VMEM_LIMIT),
        name="transforms",
    )(mine, other)


def anomaly_kernel(states_ref, pair_ref, mean_ref):
    lags, columns, levels, members = states_ref.shape
    rows = lags * columns * levels
    state = states_ref[...].reshape(rows, members).astype(F32)
    mean = jnp.mean(state, axis=1, keepdims=True)
    anomaly = (state - mean).astype(BF16).reshape(states_ref.shape)
    column = lax.broadcasted_iota(jnp.int32, states_ref.shape, 1)
    blend = jnp.abs((column.astype(F32) + 0.5) / columns - 0.5)
    pair_ref[:, :, :, :members] = anomaly
    pair_ref[:, :, :, members:] = (anomaly.astype(F32) * blend).astype(BF16)
    mean_ref[...] = jnp.broadcast_to(mean, (rows, HALF)).reshape(mean_ref.shape)


def anomalies(states):
    lags, columns, levels, members = states.shape
    block = lambda width: pl.BlockSpec((lags, HC, levels, width), lambda r: (0, r, 0, 0))
    return pl.pallas_call(
        anomaly_kernel,
        grid=(columns // HC,),
        in_specs=[block(members)],
        out_specs=[block(2 * members), block(HALF)],
        out_shape=[jax.ShapeDtypeStruct(states.shape[:-1] + (2 * members,), BF16),
                   jax.ShapeDtypeStruct(states.shape[:-1] + (HALF,), F32)],
        compiler_params=pltpu.CompilerParams(vmem_limit_bytes=VMEM_LIMIT),
        cost_estimate=pl.CostEstimate(flops=4 * states.size, bytes_accessed=8 * states.size, transcendentals=0),
        name="anomalies",
    )(states)


def update_side(region, side, lag, centre, beside, pair_ref, mean_ref, out_ref, done_ref, sem):
    levels, members = out_ref.shape[2:]
    half = HC // 2
    rows = half * levels
    cols = pl.ds(region * HC + side * half, half)
    change = (beside.astype(F32) - centre.astype(F32)).astype(BF16)
    pair = pair_ref[lag, cols].reshape(rows, 2 * members)
    moved = jnp.dot(pair, jnp.concatenate([centre, change], axis=0), preferred_element_type=F32)
    mean = mean_ref[lag, cols].reshape(rows, HALF)
    result = jnp.concatenate([mean, mean], axis=1) + moved
    done_ref[...] = result.astype(BF16).reshape(half, levels, members)
    copy = pltpu.make_async_copy(done_ref, out_ref.at[lag, cols], sem)
    copy.start()
    return copy


def update_sides(parts, pair_ref, mean_ref, out_ref, done_ref, sems):
    copies = []
    for i, (region, side, centre, beside) in enumerate(parts):
        for lag in range(out_ref.shape[0]):
            copies.append(update_side(region, side, lag, centre, beside, pair_ref, mean_ref, out_ref,
                                      done_ref.at[i, lag], sems.at[i, lag]))
    for copy in copies:
        copy.wait()


def first_update_kernel(core_ref, mine_ref, pair_ref, mean_ref, out_ref, done_ref, sems):
    core = core_ref[0]
    region = core * (pair_ref.shape[1] // HC - 1)
    near = mine_ref[1]
    parts = [(region, side, near, mine_ref[2 * side]) for side in range(2)]
    parts.append((region + 1 - 2 * core, core, mine_ref[2 - 2 * core], near))
    update_sides(parts, pair_ref, mean_ref, out_ref, done_ref, sems)


def last_update_kernel(core_ref, mine_ref, other_ref, pair_ref, mean_ref, _, out_ref, all_ref, done_ref, sems):
    core = core_ref[0]
    all_ref[pl.ds(3 * core, 3)] = mine_ref[...]
    all_ref[pl.ds(3 * (1 - core), 3)] = other_ref[...]
    regions = pair_ref.shape[1] // HC
    parts = []
    for step in range(1, regions):
        region = step + core * (regions - 1 - 2 * step)
        for side in range(2):
            if step == 1 and side == 0:
                continue
            towards = side + core * (1 - 2 * side)
            parts.append((region, towards, all_ref[region + 1], all_ref[region + 2 * towards]))
    update_sides(parts, pair_ref, mean_ref, out_ref, done_ref, sems)


def update_call(kernel, args, begun, states, count, scratch, name):
    lags, columns, levels, members = states.shape
    half = HC // 2
    vmem = pl.BlockSpec(memory_space=pltpu.VMEM)
    given = [] if begun is None else [begun]
    flops = 2 * count * lags * half * levels * 2 * members * members
    return pl.pallas_call(
        kernel,
        in_specs=[pl.BlockSpec(memory_space=pltpu.SMEM)] + [vmem] * (len(args) - 1) + [pl.BlockSpec(memory_space=pl.ANY)] * len(given),
        out_specs=pl.BlockSpec(memory_space=pl.ANY),
        out_shape=jax.ShapeDtypeStruct(states.shape, BF16),
        scratch_shapes=scratch + [pltpu.VMEM((count, lags, half, levels, members), BF16),
                                  pltpu.SemaphoreType.DMA((count, lags))],
        input_output_aliases={len(args): 0} if given else {},
        compiler_params=pltpu.CompilerParams(vmem_limit_bytes=VMEM_LIMIT),
        cost_estimate=pl.CostEstimate(flops=flops, bytes_accessed=count * lags * half * levels * members * 6, transcendentals=0),
        name=name,
    )(*args, *given)


def first_update(core, mine, pair, mean, states):
    return update_call(first_update_kernel, (core, mine, pair, mean), None, states, 3, [], "first_update")


def last_update(core, mine, other, pair, mean, begun):
    count = 2 * (begun.shape[1] // HC) - 3
    return update_call(last_update_kernel, (core, mine, other, pair, mean), begun, begun, count,
                       [pltpu.VMEM((6, K, K), BF16)], "last_update")


def shards(obs_perturb, innovation, error_weight, obs_column, obs_count, radius, states):
    core = (lax.axis_index("tm") % 2).astype(jnp.int32).reshape(1)
    spaces = lax.axis_size("space")
    terms = observation_terms(innovation, error_weight, obs_column, obs_count, radius)
    swap_core = [(0, 1), (1, 0), (2, 3), (3, 2)]
    swap_chip = [(0, 2), (2, 0), (1, 3), (3, 1)]
    up_down = []
    for chip in range(2):
        for s in range(spaces):
            following = (s + 1) % spaces
            there = 1 - chip if following % (spaces // 2) == 0 else chip
            upper, lower = (2 * chip + 1) * spaces + s, 2 * there * spaces + following
            up_down += [(upper, lower), (lower, upper)]
    send = local_grams(core, (5, 6, 7), terms, obs_perturb[0], BF16, "edges_to_send")
    recv = lax.ppermute(send, "tm", swap_core)
    keep = local_grams(1 - core, (5, 6, 7), terms, obs_perturb[0], F32, "edges_to_keep")
    edge = (keep + recv.astype(F32)).astype(BF16)
    halo = lax.ppermute(edge, ("tm", "space"), up_down)
    _, later = lax.optimization_barrier((edge, core))
    inner_send = local_grams(later, (4,), terms, obs_perturb[0], BF16, "inner_to_send")
    inner_recv = lax.ppermute(inner_send, "tm", swap_core)
    inner_keep = local_grams(1 - later, (4,), terms, obs_perturb[0], F32, "inner_to_keep")
    total, chip_sum = join_sums(core, keep, recv, inner_keep, inner_recv, halo)
    states, chip_sum = lax.optimization_barrier((states, chip_sum))
    other_chip = lax.ppermute(chip_sum, "tm", swap_chip)
    other_chip, pair, mean = lax.optimization_barrier((other_chip, *anomalies(states)))
    own = transforms(total, other_chip)
    beside = lax.ppermute(own, "tm", swap_core)
    begun = first_update(core, own, pair, mean, states)
    return last_update(core, own, beside, pair, mean, begun)


def solution(mesh):
    return jax.shard_map(
        shards,
        mesh=mesh,
        in_specs=(
            P("tm", "space", None, None),
            P("tm", "space", None),
            P("tm", "space", None),
            P("tm", "space", None),
            P("tm", "space"),
            P("space"),
            P("tm", "space", None, None),
        ),
        out_specs=P("tm", "space", None, None),
        check_vma=False,
    )
```

```python
import functools

import jax
import jax.numpy as jnp
from jax import lax
from jax.experimental import pallas as pl
from jax.experimental.pallas import tpu as pltpu
from jax.sharding import PartitionSpec as P

HC = 32
NS_ITERS = 5
INFLATION = 1.1
K = 256
HALF = K // 2
TAIL = 16
BF16 = jnp.bfloat16
F32 = jnp.float32
VMEM_LIMIT = 32 * 1024 * 1024


def row_col():
    row = lax.broadcasted_iota(jnp.int32, (HALF, HALF), 0)
    col = lax.broadcasted_iota(jnp.int32, (HALF, HALF), 1)
    return row, col


def tail_row():
    return lax.broadcasted_iota(jnp.int32, (TAIL, HALF), 0)


def observation_terms(innovation, error_weight, obs_column, obs_count, radius):
    column = obs_column[0]
    position = lax.broadcasted_iota(jnp.int32, column.shape, 1)
    base = jnp.where(position < obs_count[0][:, None], error_weight[0], 0.0)
    reach = jnp.maximum(radius[:, None], column).astype(F32)
    return base, base * innovation[0], (column.astype(F32) + (0.5 - 0.5 * HC)) / reach, HC / reach


def gram_kernel(targets, side_ref, base_ref, innov_ref, place_ref, width_ref, obs_ref, out_ref, flip_ref, weight_ref, scaled_ref):
    side = side_ref[0]
    regions = obs_ref.shape[0]
    for m in range(5):
        ratio = jnp.minimum(jnp.abs(place_ref[...] - (m - 2.0) * width_ref[...]), 1.0)
        taper = jnp.square(1.0 - ratio * ratio)
        weight_ref[m] = base_ref[...] * taper
        scaled_ref[m] = innov_ref[...] * taper
    row, col = row_col()
    tail = tail_row()
    rest = jnp.zeros((TAIL, HALF), F32)
    vecs = {}
    for r in range(regions):
        if any(0 <= t - r <= 4 for t in targets):
            flip_ref[r] = obs_ref[r + side * (regions - 1 - 2 * r)].T
    for t in reversed(targets):
        total = None
        vec = None
        for r in reversed(range(regions)):
            m = t - r
            if not 0 <= m <= 4:
                continue
            source = r + side * (regions - 1 - 2 * r)
            offset = m + side * (4 - 2 * m)
            weighted = (flip_ref[r].astype(F32) * weight_ref[offset, pl.ds(source, 1), :]).astype(BF16)
            if r not in vecs:
                here = pl.ds(source, 1)
                scaled = jnp.concatenate([scaled_ref[k, here, :] for k in (0, 1, 2, 3, 4, 4, 4, 4)], axis=0)
                high = scaled.astype(BF16)
                low = (scaled - high.astype(F32)).astype(BF16)
                weighted = jnp.concatenate([weighted, jnp.concatenate([high, low], axis=0)], axis=0)
            part = jnp.dot(weighted, obs_ref[source], preferred_element_type=F32)
            if r not in vecs:
                vecs[r] = part[K : K + 8] + part[K + 8 :]
                part = part[:K]
            total = part if total is None else total + part
            part = jnp.where(side == 0, vecs[r][m : m + 1], vecs[r][4 - m : 5 - m])
            vec = part if vec is None else vec + part
        i = t - targets[0]
        at = i + side * (len(targets) - 1 - 2 * i)
        base = pl.multiple_of(at * K, K)
        out_ref[pl.ds(base, HALF), :] = total[:HALF, HALF:].astype(out_ref.dtype)
        low = total[HALF:, HALF:]
        out_ref[pl.ds(base + HALF, HALF), :] = jnp.where(row <= col, total[:HALF, :HALF], low).astype(out_ref.dtype)
        diag = jnp.sum(jnp.where(row == col, low, 0.0), axis=0, keepdims=True)
        for k, line in enumerate((diag, vec[:, :HALF], vec[:, HALF:])):
            rest = jnp.where(tail == 3 * at + k, line, rest)
    out_ref[len(targets) * K :, :] = rest.astype(out_ref.dtype)


def local_grams(side, targets, terms, obs, dtype, name):
    regions, capacity, members = obs.shape
    vmem = pl.BlockSpec(memory_space=pltpu.VMEM)
    return pl.pallas_call(
        functools.partial(gram_kernel, targets),
        in_specs=[pl.BlockSpec(memory_space=pltpu.SMEM)] + [vmem] * 5,
        out_specs=vmem,
        out_shape=jax.ShapeDtypeStruct((len(targets) * K + TAIL, HALF), dtype),
        scratch_shapes=[pltpu.VMEM((regions, members, capacity), BF16)] + [pltpu.VMEM((5, regions, capacity), F32)] * 2,
        compiler_params=pltpu.CompilerParams(vmem_limit_bytes=VMEM_LIMIT),
        cost_estimate=pl.CostEstimate(flops=5 * regions * capacity * K * K,
                                      bytes_accessed=regions * capacity * K, transcendentals=0),
        name=name,
    )(side, *terms, obs)


def join_kernel(core_ref, edge_keep_ref, edge_recv_ref, inner_keep_ref, inner_recv_ref, halo_ref, sum_ref, send_ref):
    core = core_ref[0]
    parts = [(j + core, j + 1 - core, edge_keep_ref, edge_recv_ref) for j in range(2)]
    parts.append((2 - 2 * core, 0, inner_keep_ref, inner_recv_ref))
    for k, at, keep_ref, recv_ref in parts:
        into, of = pl.ds(pl.multiple_of(k * K, K), K), pl.ds(pl.multiple_of(at * K, K), K)
        total = keep_ref[of, :] + recv_ref[of, :].astype(F32) + halo_ref[into, :].astype(F32)
        sum_ref[into, :] = total
        send_ref[into, :] = total.astype(BF16)
    edge = edge_keep_ref[3 * K :, :] + edge_recv_ref[3 * K :, :].astype(F32)
    inner = inner_keep_ref[K:, :] + inner_recv_ref[K:, :].astype(F32)
    tail = tail_row()
    down = lambda rows, by: jnp.concatenate([rows[TAIL - by :], rows[: TAIL - by]], axis=0)
    rest = jnp.where(core == 0, jnp.where(tail < 6, down(edge, TAIL - 3), down(inner, 6)),
                     jnp.where(tail < 3, inner, down(edge, 3)))
    rest = rest + halo_ref[3 * K :, :].astype(F32)
    sum_ref[3 * K :, :] = rest
    send_ref[3 * K :, :] = rest.astype(BF16)


def join_sums(core, *sums):
    vmem = pl.BlockSpec(memory_space=pltpu.VMEM)
    return pl.pallas_call(
        join_kernel,
        in_specs=[pl.BlockSpec(memory_space=pltpu.SMEM)] + [vmem] * len(sums),
        out_specs=[vmem, vmem],
        out_shape=[jax.ShapeDtypeStruct((3 * K + TAIL, HALF), F32),
                   jax.ShapeDtypeStruct((3 * K + TAIL, HALF), BF16)],
        compiler_params=pltpu.CompilerParams(vmem_limit_bytes=2 * 1024 * 1024),
        name="join_sums",
    )(core, *sums)


def identity_mask(n):
    return lax.broadcasted_iota(jnp.int32, (n, n), 0) == lax.broadcasted_iota(jnp.int32, (n, n), 1)


def product(a, b):
    return jnp.dot(a.astype(BF16), b.astype(BF16), preferred_element_type=F32)


def transform_kernel(mine_ref, other_ref, out_ref):
    row, col = row_col()
    on_diagonal = identity_mask(K)
    count = mine_ref.shape[0] // K
    each = range(count)
    tails = mine_ref[count * K :, :] + other_ref[count * K :, :].astype(F32)
    total = lambda a: jnp.sum(jnp.sum(a, axis=0, keepdims=True), axis=1, keepdims=True)
    us, ys, frobs, shrinks, squares, vecs = [], [], [], [], [], []
    for k in each:
        packed = mine_ref[k * K : (k + 1) * K, :] + other_ref[k * K : (k + 1) * K, :].astype(F32)
        corner = packed[:HALF]
        both = packed[HALF:K] + jnp.where(row == col, (K - 1) / INFLATION, 0.0)
        rest = tails[3 * k : 3 * k + 1] + (K - 1) / INFLATION
        first = jnp.where(row == col, both, 0.0)
        mean = (total(first) + jnp.sum(rest, axis=1, keepdims=True)) * (1.0 / K)
        frob = jnp.sqrt(total(2.0 * (corner * corner + both * both) - first * first)
                        + jnp.sum(rest * rest, axis=1, keepdims=True))
        flipped = both.T
        upper = jnp.where(row <= col, both, flipped)
        lower = jnp.where(row > col, both, jnp.where(row == col, rest, flipped))
        system = jnp.concatenate(
            [jnp.concatenate([upper, corner], axis=1),
             jnp.concatenate([corner.T, lower], axis=1)], axis=0)
        u = -0.5 * (system - jnp.where(on_diagonal, mean, 0.0))
        shrink = 1.0 / frob
        us.append(u * shrink)
        ys.append(mean * shrink)
        frobs.append(frob)
        shrinks.append(shrink)
        vecs.append(jnp.concatenate([tails[3 * k + 1 : 3 * k + 2], tails[3 * k + 2 : 3 * k + 3]], axis=1))
    invs = [None for k in each]
    iotas = [1.0 for k in each]
    for iteration in range(NS_ITERS):
        last = iteration == NS_ITERS - 1
        halves = [us[k].astype(BF16) for k in each]
        if not last:
            squares = [product(halves[k], halves[k]) for k in each]
        crosses = [None if invs[k] is None else product(invs[k], halves[k]) for k in each]
        for k in each:
            u, y = us[k], ys[k]
            mu = 1.5 - 0.5 * y
            invs[k] = u if invs[k] is None else mu * invs[k] + iotas[k] * u + crosses[k]
            if not last:
                us[k] = (mu * (1.5 - 1.5 * y)) * u + (3.0 - 1.5 * y) * squares[k] + product(halves[k], squares[k])
            ys[k], iotas[k] = y * mu * mu, iotas[k] * mu
    for k in each:
        inverse = invs[k] + jnp.where(on_diagonal, iotas[k], 0.0)
        vec_col = jnp.broadcast_to(vecs[k], (HALF, K)).T[:, :1]
        half_step = jnp.sum(inverse * vec_col, axis=0, keepdims=True)
        wbar = jnp.sum(inverse * half_step, axis=1, keepdims=True) * shrinks[k]
        scale = (K - 1.0) ** 0.5 / jnp.sqrt(frobs[k])
        out_ref[k] = (scale * inverse + wbar).astype(BF16)


def transforms(mine, other):
    vmem = pl.BlockSpec(memory_space=pltpu.VMEM)
    return pl.pallas_call(
        transform_kernel,
        in_specs=[vmem, vmem],
        out_specs=vmem,
        out_shape=jax.ShapeDtypeStruct((mine.shape[0] // K, K, K), BF16),
        compiler_params=pltpu.CompilerParams(vmem_limit_bytes=VMEM_LIMIT),
        name="transforms",
    )(mine, other)


def anomaly_kernel(states_ref, pair_ref, mean_ref):
    lags, columns, levels, members = states_ref.shape
    rows = lags * columns * levels
    state = states_ref[...].reshape(rows, members).astype(F32)
    mean = jnp.mean(state, axis=1, keepdims=True)
    anomaly = (state - mean).astype(BF16).reshape(states_ref.shape)
    column = lax.broadcasted_iota(jnp.int32, states_ref.shape, 1)
    blend = jnp.abs((column.astype(F32) + 0.5) / columns - 0.5)
    pair_ref[:, :, :, :members] = anomaly
    pair_ref[:, :, :, members:] = (anomaly.astype(F32) * blend).astype(BF16)
    mean_ref[...] = jnp.broadcast_to(mean, (rows, HALF)).reshape(mean_ref.shape)


def anomalies(states):
    lags, columns, levels, members = states.shape
    block = lambda width: pl.BlockSpec((lags, HC, levels, width), lambda r: (0, r, 0, 0))
    return pl.pallas_call(
        anomaly_kernel,
        grid=(columns // HC,),
        in_specs=[block(members)],
        out_specs=[block(2 * members), block(HALF)],
        out_shape=[jax.ShapeDtypeStruct(states.shape[:-1] + (2 * members,), BF16),
                   jax.ShapeDtypeStruct(states.shape[:-1] + (HALF,), F32)],
        compiler_params=pltpu.CompilerParams(vmem_limit_bytes=VMEM_LIMIT),
        cost_estimate=pl.CostEstimate(flops=4 * states.size, bytes_accessed=8 * states.size, transcendentals=0),
        name="anomalies",
    )(states)


def update_side(region, side, lag, centre, beside, pair_ref, mean_ref, out_ref, done_ref, sem):
    levels, members = out_ref.shape[2:]
    half = HC // 2
    rows = half * levels
    cols = pl.ds(region * HC + side * half, half)
    change = (beside.astype(F32) - centre.astype(F32)).astype(BF16)
    pair = pair_ref[lag, cols].reshape(rows, 2 * members)
    moved = jnp.dot(pair, jnp.concatenate([centre, change], axis=0), preferred_element_type=F32)
    mean = mean_ref[lag, cols].reshape(rows, HALF)
    result = jnp.concatenate([mean, mean], axis=1) + moved
    done_ref[...] = result.astype(BF16).reshape(half, levels, members)
    copy = pltpu.make_async_copy(done_ref, out_ref.at[lag, cols], sem)
    copy.start()
    return copy


def update_sides(parts, pair_ref, mean_ref, out_ref, done_ref, sems):
    copies = []
    for i, (region, side, centre, beside) in enumerate(parts):
        for lag in range(out_ref.shape[0]):
            copies.append(update_side(region, side, lag, centre, beside, pair_ref, mean_ref, out_ref,
                                      done_ref.at[i, lag], sems.at[i, lag]))
    for copy in copies:
        copy.wait()


def first_update_kernel(core_ref, mine_ref, pair_ref, mean_ref, out_ref, done_ref, sems):
    core = core_ref[0]
    region = core * (pair_ref.shape[1] // HC - 1)
    near = mine_ref[1]
    parts = [(region, side, near, mine_ref[2 * side]) for side in range(2)]
    parts.append((region + 1 - 2 * core, core, mine_ref[2 - 2 * core], near))
    update_sides(parts, pair_ref, mean_ref, out_ref, done_ref, sems)


def last_update_kernel(core_ref, mine_ref, other_ref, pair_ref, mean_ref, _, out_ref, all_ref, done_ref, sems):
    core = core_ref[0]
    all_ref[pl.ds(3 * core, 3)] = mine_ref[...]
    all_ref[pl.ds(3 * (1 - core), 3)] = other_ref[...]
    regions = pair_ref.shape[1] // HC
    parts = []
    for step in range(1, regions):
        region = step + core * (regions - 1 - 2 * step)
        for side in range(2):
            if step == 1 and side == 0:
                continue
            towards = side + core * (1 - 2 * side)
            parts.append((region, towards, all_ref[region + 1], all_ref[region + 2 * towards]))
    update_sides(parts, pair_ref, mean_ref, out_ref, done_ref, sems)


def update_call(kernel, args, begun, states, count, scratch, name):
    lags, columns, levels, members = states.shape
    half = HC // 2
    vmem = pl.BlockSpec(memory_space=pltpu.VMEM)
    given = [] if begun is None else [begun]
    flops = 2 * count * lags * half * levels * 2 * members * members
    return pl.pallas_call(
        kernel,
        in_specs=[pl.BlockSpec(memory_space=pltpu.SMEM)] + [vmem] * (len(args) - 1) + [pl.BlockSpec(memory_space=pl.ANY)] * len(given),
        out_specs=pl.BlockSpec(memory_space=pl.ANY),
        out_shape=jax.ShapeDtypeStruct(states.shape, BF16),
        scratch_shapes=scratch + [pltpu.VMEM((count, lags, half, levels, members), BF16),
                                  pltpu.SemaphoreType.DMA((count, lags))],
        input_output_aliases={len(args): 0} if given else {},
        compiler_params=pltpu.CompilerParams(vmem_limit_bytes=VMEM_LIMIT),
        cost_estimate=pl.CostEstimate(flops=flops, bytes_accessed=count * lags * half * levels * members * 6, transcendentals=0),
        name=name,
    )(*args, *given)


def first_update(core, mine, pair, mean, states):
    return update_call(first_update_kernel, (core, mine, pair, mean), None, states, 3, [], "first_update")


def last_update(core, mine, other, pair, mean, begun):
    count = 2 * (begun.shape[1] // HC) - 3
    return update_call(last_update_kernel, (core, mine, other, pair, mean), begun, begun, count,
                       [pltpu.VMEM((6, K, K), BF16)], "last_update")


def shards(obs_perturb, innovation, error_weight, obs_column, obs_count, radius, states):
    core = (lax.axis_index("tm") % 2).astype(jnp.int32).reshape(1)
    spaces = lax.axis_size("space")
    terms = observation_terms(innovation, error_weight, obs_column, obs_count, radius)
    swap_core = [(0, 1), (1, 0), (2, 3), (3, 2)]
    swap_chip = [(0, 2), (2, 0), (1, 3), (3, 1)]
    up_down = []
    for chip in range(2):
        for s in range(spaces):
            following = (s + 1) % spaces
            there = 1 - chip if following % (spaces // 2) == 0 else chip
            upper, lower = (2 * chip + 1) * spaces + s, 2 * there * spaces + following
            up_down += [(upper, lower), (lower, upper)]
    send = local_grams(core, (5, 6, 7), terms, obs_perturb[0], BF16, "edges_to_send")
    recv = lax.ppermute(send, "tm", swap_core)
    keep = local_grams(1 - core, (5, 6, 7), terms, obs_perturb[0], F32, "edges_to_keep")
    edge = (keep + recv.astype(F32)).astype(BF16)
    halo = lax.ppermute(edge, ("tm", "space"), up_down)
    _, later = lax.optimization_barrier((edge, core))
    inner_send = local_grams(later, (4,), terms, obs_perturb[0], BF16, "inner_to_send")
    inner_recv = lax.ppermute(inner_send, "tm", swap_core)
    inner_keep = local_grams(1 - later, (4,), terms, obs_perturb[0], F32, "inner_to_keep")
    total, chip_sum = join_sums(core, keep, recv, inner_keep, inner_recv, halo)
    states, chip_sum = lax.optimization_barrier((states, chip_sum))
    other_chip = lax.ppermute(chip_sum, "tm", swap_chip)
    other_chip, pair, mean = lax.optimization_barrier((other_chip, *anomalies(states)))
    own = transforms(total, other_chip)
    beside = lax.ppermute(own, "tm", swap_core)
    begun = first_update(core, own, pair, mean, states)
    return last_update(core, own, beside, pair, mean, begun)


def solution(mesh):
    return jax.shard_map(
        shards,
        mesh=mesh,
        in_specs=(
            P("tm", "space", None, None),
            P("tm", "space", None),
            P("tm", "space", None),
            P("tm", "space", None),
            P("tm", "space"),
            P("space"),
            P("tm", "space", None, None),
        ),
        out_specs=P("tm", "space", None, None),
        check_vma=False,
    )
```

```python
import functools

import jax
import jax.numpy as jnp
from jax import lax
from jax.experimental import pallas as pl
from jax.experimental.pallas import tpu as pltpu
from jax.sharding import PartitionSpec as P

HC = 32
NS_ITERS = 5
INFLATION = 1.1
K = 256
HALF = K // 2
TAIL = 16
BF16 = jnp.bfloat16
F32 = jnp.float32
VMEM_LIMIT = 32 * 1024 * 1024


def row_col():
    row = lax.broadcasted_iota(jnp.int32, (HALF, HALF), 0)
    col = lax.broadcasted_iota(jnp.int32, (HALF, HALF), 1)
    return row, col


def tail_row():
    return lax.broadcasted_iota(jnp.int32, (TAIL, HALF), 0)


def observation_terms(innovation, error_weight, obs_column, obs_count, radius):
    column = obs_column[0]
    position = lax.broadcasted_iota(jnp.int32, column.shape, 1)
    base = jnp.where(position < obs_count[0][:, None], error_weight[0], 0.0)
    reach = jnp.maximum(radius[:, None], column).astype(F32)
    return base, base * innovation[0], (column.astype(F32) + (0.5 - 0.5 * HC)) / reach, HC / reach


def gram_kernel(targets, side_ref, base_ref, innov_ref, place_ref, width_ref, obs_ref, out_ref, flip_ref, weight_ref, scaled_ref):
    side = side_ref[0]
    regions = obs_ref.shape[0]
    for m in range(5):
        ratio = jnp.minimum(jnp.abs(place_ref[...] - (m - 2.0) * width_ref[...]), 1.0)
        taper = jnp.square(1.0 - ratio * ratio)
        weight_ref[m] = base_ref[...] * taper
        scaled_ref[m] = innov_ref[...] * taper
    row, col = row_col()
    tail = tail_row()
    rest = jnp.zeros((TAIL, HALF), F32)
    vecs = {}
    for r in range(regions):
        if any(0 <= t - r <= 4 for t in targets):
            flip_ref[r] = obs_ref[r + side * (regions - 1 - 2 * r)].T
    for t in reversed(targets):
        total = None
        vec = None
        for r in reversed(range(regions)):
            m = t - r
            if not 0 <= m <= 4:
                continue
            source = r + side * (regions - 1 - 2 * r)
            offset = m + side * (4 - 2 * m)
            weighted = (flip_ref[r].astype(F32) * weight_ref[offset, pl.ds(source, 1), :]).astype(BF16)
            if r not in vecs:
                here = pl.ds(source, 1)
                scaled = jnp.concatenate([scaled_ref[k, here, :] for k in (0, 1, 2, 3, 4, 4, 4, 4)], axis=0)
                high = scaled.astype(BF16)
                low = (scaled - high.astype(F32)).astype(BF16)
                weighted = jnp.concatenate([weighted, jnp.concatenate([high, low], axis=0)], axis=0)
            part = jnp.dot(weighted, obs_ref[source], preferred_element_type=F32)
            if r not in vecs:
                vecs[r] = part[K : K + 8] + part[K + 8 :]
                part = part[:K]
            total = part if total is None else total + part
            part = jnp.where(side == 0, vecs[r][m : m + 1], vecs[r][4 - m : 5 - m])
            vec = part if vec is None else vec + part
        i = t - targets[0]
        at = i + side * (len(targets) - 1 - 2 * i)
        base = pl.multiple_of(at * K, K)
        out_ref[pl.ds(base, HALF), :] = total[:HALF, HALF:].astype(out_ref.dtype)
        low = total[HALF:, HALF:]
        out_ref[pl.ds(base + HALF, HALF), :] = jnp.where(row <= col, total[:HALF, :HALF], low).astype(out_ref.dtype)
        diag = jnp.sum(jnp.where(row == col, low, 0.0), axis=0, keepdims=True)
        for k, line in enumerate((diag, vec[:, :HALF], vec[:, HALF:])):
            rest = jnp.where(tail == 3 * at + k, line, rest)
    out_ref[len(targets) * K :, :] = rest.astype(out_ref.dtype)


def local_grams(side, targets, terms, obs, dtype, name):
    regions, capacity, members = obs.shape
    vmem = pl.BlockSpec(memory_space=pltpu.VMEM)
    return pl.pallas_call(
        functools.partial(gram_kernel, targets),
        in_specs=[pl.BlockSpec(memory_space=pltpu.SMEM)] + [vmem] * 5,
        out_specs=vmem,
        out_shape=jax.ShapeDtypeStruct((len(targets) * K + TAIL, HALF), dtype),
        scratch_shapes=[pltpu.VMEM((regions, members, capacity), BF16)] + [pltpu.VMEM((5, regions, capacity), F32)] * 2,
        compiler_params=pltpu.CompilerParams(vmem_limit_bytes=VMEM_LIMIT),
        cost_estimate=pl.CostEstimate(flops=5 * regions * capacity * K * K,
                                      bytes_accessed=regions * capacity * K, transcendentals=0),
        name=name,
    )(side, *terms, obs)


def join_kernel(core_ref, edge_keep_ref, edge_recv_ref, inner_keep_ref, inner_recv_ref, halo_ref, sum_ref, send_ref):
    core = core_ref[0]
    parts = [(j + core, j + 1 - core, edge_keep_ref, edge_recv_ref) for j in range(2)]
    parts.append((2 - 2 * core, 0, inner_keep_ref, inner_recv_ref))
    for k, at, keep_ref, recv_ref in parts:
        into, of = pl.ds(pl.multiple_of(k * K, K), K), pl.ds(pl.multiple_of(at * K, K), K)
        total = keep_ref[of, :] + recv_ref[of, :].astype(F32) + halo_ref[into, :].astype(F32)
        sum_ref[into, :] = total
        send_ref[into, :] = total.astype(BF16)
    edge = edge_keep_ref[3 * K :, :] + edge_recv_ref[3 * K :, :].astype(F32)
    inner = inner_keep_ref[K:, :] + inner_recv_ref[K:, :].astype(F32)
    tail = tail_row()
    down = lambda rows, by: jnp.concatenate([rows[TAIL - by :], rows[: TAIL - by]], axis=0)
    rest = jnp.where(core == 0, jnp.where(tail < 6, down(edge, TAIL - 3), down(inner, 6)),
                     jnp.where(tail < 3, inner, down(edge, 3)))
    rest = rest + halo_ref[3 * K :, :].astype(F32)
    sum_ref[3 * K :, :] = rest
    send_ref[3 * K :, :] = rest.astype(BF16)


def join_sums(core, *sums):
    vmem = pl.BlockSpec(memory_space=pltpu.VMEM)
    return pl.pallas_call(
        join_kernel,
        in_specs=[pl.BlockSpec(memory_space=pltpu.SMEM)] + [vmem] * len(sums),
        out_specs=[vmem, vmem],
        out_shape=[jax.ShapeDtypeStruct((3 * K + TAIL, HALF), F32),
                   jax.ShapeDtypeStruct((3 * K + TAIL, HALF), BF16)],
        compiler_params=pltpu.CompilerParams(vmem_limit_bytes=2 * 1024 * 1024),
        name="join_sums",
    )(core, *sums)


def identity_mask(n):
    return lax.broadcasted_iota(jnp.int32, (n, n), 0) == lax.broadcasted_iota(jnp.int32, (n, n), 1)


def product(a, b):
    return jnp.dot(a.astype(BF16), b.astype(BF16), preferred_element_type=F32)


def transform_kernel(mine_ref, other_ref, out_ref):
    row, col = row_col()
    on_diagonal = identity_mask(K)
    count = mine_ref.shape[0] // K
    each = range(count)
    tails = mine_ref[count * K :, :] + other_ref[count * K :, :].astype(F32)
    total = lambda a: jnp.sum(jnp.sum(a, axis=0, keepdims=True), axis=1, keepdims=True)
    us, ys, frobs, shrinks, squares, vecs = [], [], [], [], [], []
    for k in each:
        packed = mine_ref[k * K : (k + 1) * K, :] + other_ref[k * K : (k + 1) * K, :].astype(F32)
        corner = packed[:HALF]
        both = packed[HALF:K] + jnp.where(row == col, (K - 1) / INFLATION, 0.0)
        rest = tails[3 * k : 3 * k + 1] + (K - 1) / INFLATION
        first = jnp.where(row == col, both, 0.0)
        mean = (total(first) + jnp.sum(rest, axis=1, keepdims=True)) * (1.0 / K)
        frob = jnp.sqrt(total(2.0 * (corner * corner + both * both) - first * first)
                        + jnp.sum(rest * rest, axis=1, keepdims=True))
        flipped = both.T
        upper = jnp.where(row <= col, both, flipped)
        lower = jnp.where(row > col, both, jnp.where(row == col, rest, flipped))
        system = jnp.concatenate(
            [jnp.concatenate([upper, corner], axis=1),
             jnp.concatenate([corner.T, lower], axis=1)], axis=0)
        u = -0.5 * (system - jnp.where(on_diagonal, mean, 0.0))
        shrink = 1.0 / frob
        us.append(u * shrink)
        ys.append(mean * shrink)
        frobs.append(frob)
        shrinks.append(shrink)
        vecs.append(jnp.concatenate([tails[3 * k + 1 : 3 * k + 2], tails[3 * k + 2 : 3 * k + 3]], axis=1))
    invs = [None for k in each]
    iotas = [1.0 for k in each]
    for iteration in range(NS_ITERS):
        last = iteration == NS_ITERS - 1
        halves = [us[k].astype(BF16) for k in each]
        if not last:
            squares = [product(halves[k], halves[k]) for k in each]
        crosses = [None if invs[k] is None else product(invs[k], halves[k]) for k in each]
        for k in each:
            u, y = us[k], ys[k]
            mu = 1.5 - 0.5 * y
            invs[k] = u if invs[k] is None else mu * invs[k] + iotas[k] * u + crosses[k]
            if not last:
                us[k] = (mu * (1.5 - 1.5 * y)) * u + (3.0 - 1.5 * y) * squares[k] + product(halves[k], squares[k])
            ys[k], iotas[k] = y * mu * mu, iotas[k] * mu
    for k in each:
        inverse = invs[k] + jnp.where(on_diagonal, iotas[k], 0.0)
        vec_col = jnp.broadcast_to(vecs[k], (8, K)).T[:, :1]
        half_step = jnp.sum(inverse * vec_col, axis=0, keepdims=True)
        wbar = jnp.sum(inverse * half_step, axis=1, keepdims=True) * shrinks[k]
        scale = (K - 1.0) ** 0.5 / jnp.sqrt(frobs[k])
        out_ref[k] = (scale * inverse + wbar).astype(BF16)


def transforms(mine, other):
    vmem = pl.BlockSpec(memory_space=pltpu.VMEM)
    return pl.pallas_call(
        transform_kernel,
        in_specs=[vmem, vmem],
        out_specs=vmem,
        out_shape=jax.ShapeDtypeStruct((mine.shape[0] // K, K, K), BF16),
        compiler_params=pltpu.CompilerParams(vmem_limit_bytes=VMEM_LIMIT),
        name="transforms",
    )(mine, other)


def anomaly_kernel(states_ref, pair_ref, mean_ref):
    lags, columns, levels, members = states_ref.shape
    rows = lags * columns * levels
    state = states_ref[...].reshape(rows, members).astype(F32)
    mean = jnp.mean(state, axis=1, keepdims=True)
    anomaly = (state - mean).astype(BF16).reshape(states_ref.shape)
    column = lax.broadcasted_iota(jnp.int32, states_ref.shape, 1)
    blend = jnp.abs((column.astype(F32) + 0.5) / columns - 0.5)
    pair_ref[:, :, :, :members] = anomaly
    pair_ref[:, :, :, members:] = (anomaly.astype(F32) * blend).astype(BF16)
    mean_ref[...] = jnp.broadcast_to(mean, (rows, HALF)).reshape(mean_ref.shape)


def anomalies(states):
    lags, columns, levels, members = states.shape
    block = lambda width: pl.BlockSpec((lags, HC, levels, width), lambda r: (0, r, 0, 0))
    return pl.pallas_call(
        anomaly_kernel,
        grid=(columns // HC,),
        in_specs=[block(members)],
        out_specs=[block(2 * members), block(HALF)],
        out_shape=[jax.ShapeDtypeStruct(states.shape[:-1] + (2 * members,), BF16),
                   jax.ShapeDtypeStruct(states.shape[:-1] + (HALF,), F32)],
        compiler_params=pltpu.CompilerParams(vmem_limit_bytes=VMEM_LIMIT),
        cost_estimate=pl.CostEstimate(flops=4 * states.size, bytes_accessed=8 * states.size, transcendentals=0),
        name="anomalies",
    )(states)


def update_side(region, side, lag, centre, beside, pair_ref, mean_ref, out_ref, done_ref, sem):
    levels, members = out_ref.shape[2:]
    half = HC // 2
    rows = half * levels
    cols = pl.ds(region * HC + side * half, half)
    change = (beside.astype(F32) - centre.astype(F32)).astype(BF16)
    pair = pair_ref[lag, cols].reshape(rows, 2 * members)
    moved = jnp.dot(pair, jnp.concatenate([centre, change], axis=0), preferred_element_type=F32)
    mean = mean_ref[lag, cols].reshape(rows, HALF)
    result = jnp.concatenate([mean, mean], axis=1) + moved
    done_ref[...] = result.astype(BF16).reshape(half, levels, members)
    copy = pltpu.make_async_copy(done_ref, out_ref.at[lag, cols], sem)
    copy.start()
    return copy


def update_sides(parts, pair_ref, mean_ref, out_ref, done_ref, sems):
    copies = []
    for i, (region, side, centre, beside) in enumerate(parts):
        for lag in range(out_ref.shape[0]):
            copies.append(update_side(region, side, lag, centre, beside, pair_ref, mean_ref, out_ref,
                                      done_ref.at[i, lag], sems.at[i, lag]))
    for copy in copies:
        copy.wait()


def first_update_kernel(core_ref, mine_ref, pair_ref, mean_ref, out_ref, done_ref, sems):
    core = core_ref[0]
    region = core * (pair_ref.shape[1] // HC - 1)
    near = mine_ref[1]
    parts = [(region, side, near, mine_ref[2 * side]) for side in range(2)]
    parts.append((region + 1 - 2 * core, core, mine_ref[2 - 2 * core], near))
    update_sides(parts, pair_ref, mean_ref, out_ref, done_ref, sems)


def last_update_kernel(core_ref, mine_ref, other_ref, pair_ref, mean_ref, _, out_ref, all_ref, done_ref, sems):
    core = core_ref[0]
    all_ref[pl.ds(3 * core, 3)] = mine_ref[...]
    all_ref[pl.ds(3 * (1 - core), 3)] = other_ref[...]
    regions = pair_ref.shape[1] // HC
    parts = []
    for step in range(1, regions):
        region = step + core * (regions - 1 - 2 * step)
        for side in range(2):
            if step == 1 and side == 0:
                continue
            towards = side + core * (1 - 2 * side)
            parts.append((region, towards, all_ref[region + 1], all_ref[region + 2 * towards]))
    update_sides(parts, pair_ref, mean_ref, out_ref, done_ref, sems)


def update_call(kernel, args, begun, states, count, scratch, name):
    lags, columns, levels, members = states.shape
    half = HC // 2
    vmem = pl.BlockSpec(memory_space=pltpu.VMEM)
    given = [] if begun is None else [begun]
    flops = 2 * count * lags * half * levels * 2 * members * members
    return pl.pallas_call(
        kernel,
        in_specs=[pl.BlockSpec(memory_space=pltpu.SMEM)] + [vmem] * (len(args) - 1) + [pl.BlockSpec(memory_space=pl.ANY)] * len(given),
        out_specs=pl.BlockSpec(memory_space=pl.ANY),
        out_shape=jax.ShapeDtypeStruct(states.shape, BF16),
        scratch_shapes=scratch + [pltpu.VMEM((count, lags, half, levels, members), BF16),
                                  pltpu.SemaphoreType.DMA((count, lags))],
        input_output_aliases={len(args): 0} if given else {},
        compiler_params=pltpu.CompilerParams(vmem_limit_bytes=VMEM_LIMIT),
        cost_estimate=pl.CostEstimate(flops=flops, bytes_accessed=count * lags * half * levels * members * 6, transcendentals=0),
        name=name,
    )(*args, *given)


def first_update(core, mine, pair, mean, states):
    return update_call(first_update_kernel, (core, mine, pair, mean), None, states, 3, [], "first_update")


def last_update(core, mine, other, pair, mean, begun):
    count = 2 * (begun.shape[1] // HC) - 3
    return update_call(last_update_kernel, (core, mine, other, pair, mean), begun, begun, count,
                       [pltpu.VMEM((6, K, K), BF16)], "last_update")


def shards(obs_perturb, innovation, error_weight, obs_column, obs_count, radius, states):
    core = (lax.axis_index("tm") % 2).astype(jnp.int32).reshape(1)
    spaces = lax.axis_size("space")
    terms = observation_terms(innovation, error_weight, obs_column, obs_count, radius)
    swap_core = [(0, 1), (1, 0), (2, 3), (3, 2)]
    swap_chip = [(0, 2), (2, 0), (1, 3), (3, 1)]
    up_down = []
    for chip in range(2):
        for s in range(spaces):
            following = (s + 1) % spaces
            there = 1 - chip if following % (spaces // 2) == 0 else chip
            upper, lower = (2 * chip + 1) * spaces + s, 2 * there * spaces + following
            up_down += [(upper, lower), (lower, upper)]
    send = local_grams(core, (5, 6, 7), terms, obs_perturb[0], BF16, "edges_to_send")
    recv = lax.ppermute(send, "tm", swap_core)
    keep = local_grams(1 - core, (5, 6, 7), terms, obs_perturb[0], F32, "edges_to_keep")
    edge = (keep + recv.astype(F32)).astype(BF16)
    halo = lax.ppermute(edge, ("tm", "space"), up_down)
    _, later = lax.optimization_barrier((edge, core))
    inner_send = local_grams(later, (4,), terms, obs_perturb[0], BF16, "inner_to_send")
    inner_recv = lax.ppermute(inner_send, "tm", swap_core)
    inner_keep = local_grams(1 - later, (4,), terms, obs_perturb[0], F32, "inner_to_keep")
    total, chip_sum = join_sums(core, keep, recv, inner_keep, inner_recv, halo)
    states, chip_sum = lax.optimization_barrier((states, chip_sum))
    other_chip = lax.ppermute(chip_sum, "tm", swap_chip)
    other_chip, pair, mean = lax.optimization_barrier((other_chip, *anomalies(states)))
    own = transforms(total, other_chip)
    beside = lax.ppermute(own, "tm", swap_core)
    begun = first_update(core, own, pair, mean, states)
    return last_update(core, own, beside, pair, mean, begun)


def solution(mesh):
    return jax.shard_map(
        shards,
        mesh=mesh,
        in_specs=(
            P("tm", "space", None, None),
            P("tm", "space", None),
            P("tm", "space", None),
            P("tm", "space", None),
            P("tm", "space"),
            P("space"),
            P("tm", "space", None, None),
        ),
        out_specs=P("tm", "space", None, None),
        check_vma=False,
    )
```
